32 devices in a mesh: row: 2 (over x), col: 16 (over z, y, core).
Axes of the slice: x: 2, y: 2, z: 4, core: 2. Of those that a mesh axis runs over, the one named last changes fastest.
Arguments:
- layer_input: bfloat16 [5120, 3072], P(('row', 'col')), may hold values from -0.119628906 to 0.119628906
- queries: bfloat16 [5120, 128], P(('row', 'col')), may hold values from -7 to 7
- key_states: bfloat16 [5120, 128], P(('row', 'col')), may hold values from -7 to 7
- value_states: bfloat16 [5120, 128], P(('row', 'col')), may hold values from -6 to 6
- forward_out: bfloat16 [5120, 128], P(('row', 'col')), may hold values from -1.5 to 1.5
- out_grad: bfloat16 [5120, 128], P(('row', 'col')), may hold values from -12 to 12
- token_pos: int32 [5120], replicated, may hold values from 0 to 5119, as said below
- block_sample: int32 [40], replicated, may hold values from 0 to 4, never falling along the last dimension, each value on 1 to 20 neighbouring positions
Outputs:
- query_grad: bfloat16 [5120, 128], P(('row', 'col'))
- key_grad: bfloat16 [5120, 128], P(('row', 'col'))
- value_grad: bfloat16 [5120, 128], P(('row', 'col'))
- weight_grad: float32 [3072, 384], P('col')
The draws below stay inside these ranges and needn't reach their ends.
Inputs may be any that keep to these rules, and one draw needn't show every extreme that they name: `token_pos`: each packed position appears in exactly one slot. `block_sample`: never falling along the blocks; every sample spans 1 to 20 blocks and one spans exactly 20.
All inputs are finite; a program needn't handle non-finite values.
Results may differ from the reference program's by a relative error of at most 0.019.
Values may be sent and summed in bfloat16 or wider, within the bound.
No kernel may reach another device: no remote copies, remote signals or barrier semaphores. Data moves between devices by JAX's collectives and lax.ppermute only.
A program may use at most 64 MiB of HBM per device.

```python
import math
import jax
import jax.numpy as jnp
import numpy as np
from jax import lax

D = 3072
HD = 128
TOK_DEV = 160
BLK = 128
S = 5120
TOKQ = 2560
TOKK = 320
NBLK = 40
N_ROW = 2
N_COL = 16


def slot_positions(key):
    return jax.random.permutation(jax.random.fold_in(key, 7), S).astype(jnp.int32)


def draw_token_pos(key, part):
    return slot_positions(key)


def draw_queries(key, part):
    base_key = jax.random.fold_in(key, 21)
    values = jnp.clip(1.2 * jax.random.normal(base_key, (S, HD), jnp.float32), -7.0, 7.0)
    return values.astype(jnp.bfloat16)


def draw_key_states(key, part):
    base_key = jax.random.fold_in(key, 22)
    values = jnp.clip(1.2 * jax.random.normal(base_key, (S, HD), jnp.float32), -7.0, 7.0)
    return values.astype(jnp.bfloat16)


def with_spikes(entries, rng, source, target, blocks, factor):
    def block_of(dim):
        return (jnp.arange(entries.shape[dim]) // (entries.shape[dim] // blocks)).reshape((-1,) + (1,) * (entries.ndim - 1 - dim))

    one_side = jax.random.permutation(rng, blocks)[block_of(target)]
    other_side = (block_of(target) + blocks // 2) % blocks
    return jnp.where((block_of(source) == one_side) | (block_of(source) == other_side), factor * entries, entries)


def block_scale(stream_key, extent, pieces, low, largest):
    def one(position, shards_of):
        steps = jax.random.uniform(jax.random.fold_in(jax.random.fold_in(stream_key, 6), position), (shards_of,), jnp.float32, low / len(pieces), largest / len(pieces))
        return jnp.repeat(jnp.exp(steps), extent[position] // shards_of).reshape((-1,) + (1,) * (len(extent) - position - 1))

    level = one(*pieces[0])
    for cut in pieces[1:]:
        level = level * one(*cut)
    return level


def length_profile(number_of, total, reach, slope):
    weights = [(1 << 20) // math.isqrt(grade ** slope) + 1 for grade in range(2, number_of + 1)]
    spare, given = total - reach - (number_of - 1), [1] * (number_of - 1)
    while spare > 0:
        free = [i for i in range(number_of - 1) if given[i] < reach]
        whole, left = sum([weights[i] for i in free]), spare
        for i in free:
            more = min(reach - given[i], max(1, left * weights[i] // whole), spare)
            given[i] = given[i] + more
            spare = spare - more
    return np.array([reach] + given)


def uneven(own_key, amount, total, most, skew):
    if amount == 2:
        one = jax.random.randint(own_key, (), max(1, total - most), min(most, total - 1) + 1)
        return jnp.stack([one, total - one])
    tallies = jnp.asarray(length_profile(amount, total, most, skew), jnp.int32)
    couples = (amount - 1) // 2
    giver, taker = tallies[1:1 + 2 * couples:2], tallies[2:2 + 2 * couples:2]
    slack = jnp.minimum(giver - 1, most - taker)
    shifted = jax.random.randint(jax.random.fold_in(own_key, 1), (couples,), 0, 1 << 20) % (slack + 1)
    tallies = tallies.at[1:1 + 2 * couples:2].set(giver - shifted).at[2:2 + 2 * couples:2].set(taker + shifted)
    return tallies[jax.random.permutation(jax.random.fold_in(own_key, 2), amount)]


def centred(stream_key, shape, scale, bound, cuts=(), kind=jnp.bfloat16):
    drawn = jax.random.normal(stream_key, shape, jnp.float32) * scale
    if len(cuts) > 0:
        drawn = block_scale(stream_key, shape, cuts, -0.22, 0.18) * drawn
    return jnp.clip(drawn, min=-bound, max=bound).astype(kind)


def heavy_noise(key, extent, spread, limit, cuts, heavy, kind=jnp.bfloat16):
    values = spread * jax.random.normal(key, extent, jnp.float32)
    if cuts:
        values = values * block_scale(key, extent, cuts, -0.22, 0.18)
    return jnp.clip(with_spikes(values, jax.random.fold_in(key, 3), *heavy), -limit, limit).astype(kind)


def setup_inputs(seed: int = 0) -> dict:
    arg_keys = jax.random.split(jax.random.key(seed), 9)
    return {
        "layer_input": heavy_noise(arg_keys[0], (S, D), 0.02, 0.119628906, ((0, 32),), (0, 1, 32, 2.75)),
        "queries": draw_queries(jax.random.fold_in(arg_keys[8], 71), 0),
        "key_states": draw_key_states(jax.random.fold_in(arg_keys[8], 71), 0),
        "value_states": centred(arg_keys[3], (S, HD), 1.0, 6.0, ((0, 32),)),
        "forward_out": centred(arg_keys[4], (S, HD), 0.25, 1.5, ((0, 32),)),
        "out_grad": centred(arg_keys[5], (S, HD), 2.0, 12.0, ((0, 32),)),
        "token_pos": draw_token_pos(jax.random.fold_in(arg_keys[8], 71), 0),
        "block_sample": jnp.searchsorted(jnp.cumsum(uneven(arg_keys[7], NBLK // 8, NBLK, min(32, NBLK // 2), 2)), jnp.arange(NBLK), side="right").astype(jnp.int32),
    }


NEG_FILL = -1e30


def rounded(values):
    return lax.optimization_barrier(values.astype(jnp.bfloat16)).astype(jnp.float32)


def reference(layer_input, queries, key_states, value_states, forward_out, out_grad, token_pos, block_sample):
    score_scale = 1.0 / (HD ** 0.5)
    sample_ids = jnp.take(block_sample, (token_pos // BLK).astype(jnp.int32))
    row_delta = jnp.sum(out_grad.astype(jnp.float32) * forward_out.astype(jnp.float32), axis=1)

    def by_row(array):
        return array.reshape((N_ROW, TOKQ) + array.shape[1:])

    def by_col(array):
        grouped = array.reshape((N_ROW, N_COL, TOK_DEV) + array.shape[1:])
        return jnp.swapaxes(grouped, 0, 1).reshape((N_COL, TOKK) + array.shape[1:])

    col_keys = by_col(key_states)
    col_values = by_col(value_states)
    col_samples = by_col(sample_ids)

    def row_step(running, row_inputs):
        key_acc, value_acc = running
        query_rows, grad_rows, delta_rows, query_samples = row_inputs

        def masked(key_rows, key_samples):
            scores = jnp.dot(query_rows, key_rows.T, preferred_element_type=jnp.float32) * score_scale
            live_pairs = query_samples[:, None] == key_samples[None, :]
            return jnp.where(live_pairs, scores, NEG_FILL), live_pairs

        def stat_step(stats, col_inputs):
            old_peak, row_sum = stats
            scores, live_pairs = masked(col_inputs[0], col_inputs[1])
            new_peak = jnp.maximum(old_peak, jnp.max(scores, axis=1))
            fresh = jnp.sum(jnp.where(live_pairs, jnp.exp(scores - new_peak[:, None]), 0.0), axis=1)
            return (new_peak, row_sum * jnp.exp(old_peak - new_peak) + fresh), None

        start_stats = (jnp.full((TOKQ,), NEG_FILL, jnp.float32), jnp.zeros((TOKQ,), jnp.float32))
        (row_peak, row_total), unused = lax.scan(stat_step, start_stats, (col_keys, col_samples))

        def grad_step(query_acc, col_inputs):
            key_rows, value_rows, key_samples = col_inputs
            scores, live_pairs = masked(key_rows, key_samples)
            prob_rows = jnp.where(live_pairs, jnp.exp(scores - row_peak[:, None]), 0.0) / row_total[:, None]
            prob_low = prob_rows.astype(jnp.bfloat16)
            value_part = jnp.dot(prob_low.T, grad_rows, preferred_element_type=jnp.float32)
            prob_grad = jnp.dot(grad_rows, value_rows.T, preferred_element_type=jnp.float32)
            score_grad = (prob_rows * (prob_grad - delta_rows[:, None])).astype(jnp.bfloat16)
            query_part = jnp.dot(score_grad, key_rows, preferred_element_type=jnp.float32) * score_scale
            key_part = jnp.dot(score_grad.T, query_rows, preferred_element_type=jnp.float32) * score_scale
            return query_acc + rounded(query_part), (rounded(key_part), rounded(value_part))

        query_acc, (key_parts, value_parts) = lax.scan(
            grad_step, jnp.zeros((TOKQ, HD), jnp.float32), (col_keys, col_values, col_samples))
        return (key_acc + key_parts, value_acc + value_parts), query_acc.astype(jnp.bfloat16)

    zero_acc = jnp.zeros((N_COL, TOKK, HD), jnp.float32)
    (key_acc, value_acc), query_grad = lax.scan(
        row_step, (zero_acc, zero_acc),
        (by_row(queries), by_row(out_grad), by_row(row_delta), by_row(sample_ids)))
    query_grad = query_grad.reshape(S, HD)

    def unpack(acc):
        return jnp.swapaxes(acc.reshape(N_COL, N_ROW, TOK_DEV, HD), 0, 1).reshape(S, HD).astype(jnp.bfloat16)

    key_grad = unpack(key_acc)
    value_grad = unpack(value_acc)
    all_grads = jnp.concatenate([query_grad, key_grad, value_grad], axis=1)
    weight_grad = jnp.dot(layer_input.T, all_grads, preferred_element_type=jnp.float32)
    return query_grad, key_grad, value_grad, weight_grad
```

```python
import functools
import math

import jax
import jax.numpy as jnp
from jax import lax
from jax.experimental import pallas as pl
from jax.experimental.pallas import tpu as pltpu
from jax.sharding import Mesh
from jax.sharding import PartitionSpec as P

BLK = 128
LANES = 128
PAD_ROWS = 16
NEG_FILL = -1e30
LOG2E = math.log2(math.e)
MIB = 1 << 20
F32 = jnp.float32
BF16 = jnp.bfloat16
VMEM = pl.BlockSpec(memory_space=pltpu.VMEM)
SMEM = pl.BlockSpec(memory_space=pltpu.SMEM)


def dot_nt(left, right, precision=None):
    return lax.dot_general(
        left, right, (((1,), (1,)), ((), ())), preferred_element_type=F32, precision=precision
    )


def dot_tn(left, right):
    return lax.dot_general(left, right, (((0,), (0,)), ((), ())), preferred_element_type=F32)


def params(nbytes):
    return pltpu.CompilerParams(vmem_limit_bytes=nbytes)


def split_three(values):
    high = values.astype(BF16).astype(F32)
    rest = values - high
    middle = rest.astype(BF16).astype(F32)
    return high, middle, rest - middle


def pack_kernel(axes, q_ref, k_ref, v_ref, o_ref, g_ref, pos_ref, ids_ref, qg_ref, kv_ref, prod, extra):
    count, width = q_ref.shape
    me = jnp.int32(0)
    for name, size in axes:
        me = me * size + lax.axis_index(name)
    qg_ref[:count, :width] = q_ref[...]
    qg_ref[:count, width:] = g_ref[...]
    kv_ref[:count, :width] = k_ref[...]
    kv_ref[:count, width:] = v_ref[...]
    prod[...] = jnp.zeros_like(prod)
    prod[:count, :] = g_ref[...].astype(F32) * o_ref[...].astype(F32)
    delta = dot_nt(
        jnp.ones((PAD_ROWS, width), F32), prod[...], precision=lax.Precision.HIGHEST
    )
    high, middle, low = split_three(delta)
    row = lax.broadcasted_iota(jnp.int32, delta.shape, 0)
    extra[...] = jnp.where(row == 0, high, jnp.where(row == 1, middle, jnp.where(row == 2, low, 0.0)))
    block = pos_ref[pl.ds(me, 1), :] // BLK

    def add_id(index, found):
        return jnp.where(block == index, ids_ref[index], found)

    found = lax.fori_loop(0, ids_ref.shape[0], add_id, jnp.zeros_like(block))
    extra[3:4, :count] = found.astype(F32)
    tail = extra[...].astype(BF16)
    qg_ref[count:, :] = tail
    kv_ref[count:, :] = tail


def forward_kernel(count, width, n_q, n_kv, *refs):
    qg_refs, refs = refs[:n_q], refs[n_q:]
    kv_refs, refs = refs[:n_kv], refs[n_kv:]
    w_ref, u_ref, stat_ref, own_ref, refs = *refs[:4], refs[4:]
    send_refs, (queries, grads, keys, rows) = refs[: n_q - 1], refs[n_q - 1 :]
    total = n_q * count
    factor = LOG2E / math.sqrt(width)
    for slot, ref in enumerate(qg_refs):
        queries[slot * count : (slot + 1) * count, :] = ref[:count, :width]
        grads[slot * count : (slot + 1) * count, :] = ref[:count, width:]
        tail = ref[count:, :].astype(F32)
        rows[0:1, slot * count : (slot + 1) * count] = (tail[0:1] + tail[1:2] + tail[2:3])[:, :count]
        rows[1:2, slot * count : (slot + 1) * count] = tail[3:4, :count]
    delta = rows[0:1, :]
    query_ids = rows[1:2, :]

    def over_pieces(body, state):
        base = 0
        for ref in kv_refs:
            depth = ref.shape[0]
            if depth == 1:
                state = body(ref.at[0], base, state)
            else:
                state = lax.fori_loop(
                    0, depth, lambda i, s, ref=ref, base=base: body(ref.at[i], base + i, s), state
                )
            base += depth
        return state

    def scores_of(ref):
        key_ids = jnp.transpose(ref[count:, :].astype(F32))[:count, 3:4]
        scores = dot_nt(ref[:count, :width], queries[...]) * factor
        return jnp.where(key_ids == query_ids, scores, NEG_FILL)

    def fold(values, combine):
        out = values[0:8]
        for start in range(8, count, 8):
            out = combine(out, values[start : start + 8])
        return out

    def peak_step(ref, index, peak):
        return jnp.maximum(peak, fold(scores_of(ref), jnp.maximum))

    peak8 = over_pieces(peak_step, jnp.full((8, total), NEG_FILL, F32))
    peak = jnp.max(peak8, axis=0, keepdims=True)

    def grad_step(ref, index, mass):
        weight = jnp.exp2(scores_of(ref) - peak)
        w_ref[index] = weight.astype(BF16)
        prob_grad = dot_nt(ref[:count, width:], grads[...])
        u_ref[index] = (weight * (prob_grad - delta)).astype(BF16)
        keys[index] = ref[:count, :width]
        return mass + fold(weight, jnp.add)

    mass8 = over_pieces(grad_step, jnp.zeros((8, total), F32))
    mass = jnp.sum(mass8, axis=0, keepdims=True)
    level = peak + jnp.log2(mass)
    stat_ref[...] = jnp.zeros_like(stat_ref)
    stat_ref[0:1, :] = peak
    stat_ref[1:2, :] = level

    n_pieces = keys.shape[0]
    if n_pieces <= 8:
        joined = dot_tn(
            keys[...].reshape(n_pieces * count, width), u_ref[...].reshape(n_pieces * count, total)
        )
    else:
        joined = lax.fori_loop(
            0,
            n_pieces,
            lambda i, s: s + dot_tn(keys[i], u_ref[i]),
            jnp.zeros((width, total), F32),
        )
    query_part = jnp.transpose(joined / mass)
    own_ref[...] = query_part[:count]
    chunks = total // LANES
    parts = split_three(level)
    tail_rows = send_refs[0].shape[0] - count
    lines = [part[:, c * LANES : (c + 1) * LANES] for part in parts for c in range(chunks)]
    row = lax.broadcasted_iota(jnp.int32, (tail_rows, LANES), 0)
    tail = jnp.zeros((tail_rows, LANES), F32)
    for place, line in enumerate(lines):
        tail = jnp.where(row == place, line, tail)
    tail = tail.astype(BF16)
    for slot, ref in enumerate(send_refs, 1):
        ref[:count, :] = query_part[slot * count : (slot + 1) * count].astype(BF16)
        ref[count:, :] = tail


def backward_kernel(count, width, n_q, *refs):
    w_ref, u_ref, stat_ref, own_ref, refs = *refs[:4], refs[4:]
    qg_refs, refs = refs[:n_q], refs[n_q:]
    got_refs, refs = refs[: n_q - 1], refs[n_q - 1 :]
    mine_ref, other_ref, dq_ref, queries, grads = refs
    total = n_q * count
    chunks = total // LANES
    scale = 1.0 / math.sqrt(width)
    stat = jnp.transpose(stat_ref[...])
    peak, level = stat[:, 0:1], stat[:, 1:2]
    levels = [[level[s * count : (s + 1) * count] for s in range(n_q)]]
    for offset, ref in enumerate(got_refs, 1):
        tail = ref[count:, :].astype(F32)
        summed = tail[:chunks] + tail[chunks : 2 * chunks] + tail[2 * chunks : 3 * chunks]
        summed = jnp.concatenate([summed, jnp.zeros((-chunks % 8, LANES), F32)], axis=0)
        across = jnp.transpose(summed)
        column = jnp.concatenate([across[:, c : c + 1] for c in range(chunks)], axis=0)
        levels.append(
            [column[(s ^ offset) * count : ((s ^ offset) + 1) * count] for s in range(n_q)]
        )
    for slot in range(n_q):
        here = [one[slot] for one in levels]
        top = functools.reduce(jnp.maximum, here)
        shares = [jnp.exp2(one - top) for one in here]
        mass = functools.reduce(jnp.add, shares)
        rows = slice(slot * count, (slot + 1) * count)
        share = jnp.exp2(peak[rows] - top) / mass
        queries[rows, :] = (qg_refs[slot][:count, :width].astype(F32) * share).astype(BF16)
        grads[rows, :] = (qg_refs[slot][:count, width:].astype(F32) * share).astype(BF16)
        if slot == 0:
            query_grad = own_ref[...] * shares[0]
            for one, ref in zip(shares[1:], got_refs):
                query_grad = query_grad + ref[:count, :].astype(F32) * one
            dq_ref[...] = (query_grad * (scale / mass)).astype(BF16)

    n_pieces = w_ref.shape[0]
    half = n_pieces // 2

    def emit(first, size, ref, place):
        many = (size * count, total)
        value_part = jnp.dot(
            w_ref[pl.ds(first, size)].reshape(many), grads[...], preferred_element_type=F32
        )
        key_part = jnp.dot(
            u_ref[pl.ds(first, size)].reshape(many), queries[...], preferred_element_type=F32
        )
        shape = (size, count, width)
        ref[pl.ds(place, size), :, :width] = (key_part * scale).reshape(shape).astype(ref.dtype)
        ref[pl.ds(place, size), :, width:] = value_part.reshape(shape).astype(ref.dtype)

    if half <= 4:
        emit(half, half, other_ref, 0)
        emit(0, half, mine_ref, 0)
    else:

        @pl.loop(0, half)
        def _(i):
            emit(half + i, 1, other_ref, i)
            emit(i, 1, mine_ref, i)


def weight_kernel(n_pairs, *refs):
    x_refs, refs = refs[:n_pairs], refs[n_pairs:]
    g_refs, refs = refs[:n_pairs], refs[n_pairs:]
    mine_ref, other_ref, sums = refs
    total = None
    for x_ref, g_ref in zip(x_refs, g_refs):
        part = dot_tn(x_ref[...], g_ref[...])
        total = part if total is None else total + part
    sums[...] = total.reshape(sums.shape)
    z_id, core_id = lax.axis_index("z"), lax.axis_index("core")
    for slot in range(sums.shape[1]):
        mine_ref[slot] = sums[core_id, z_id ^ slot]
        other_ref[slot] = sums[core_id ^ 1, z_id ^ slot].astype(other_ref.dtype)


def xor_permute(value, names, offsets):
    sizes = [lax.axis_size(name) for name in names]
    pairs = []
    for source in range(math.prod(sizes)):
        rest, digits = source, []
        for size in reversed(sizes):
            digits.append(rest % size)
            rest //= size
        target = 0
        for digit, size, offset in zip(reversed(digits), sizes, offsets):
            target = target * size + (digit ^ offset)
        pairs.append((source, target))
    return lax.ppermute(value, tuple(names), pairs)


def local(axes, layer_input, queries, keys, values, forward_out, out_grad, token_pos, block_sample):
    sizes = dict(axes)
    n_row, n_z, n_y, n_core = (sizes[name] for name in ("row", "z", "y", "core"))
    count, width = queries.shape
    model_width = layer_input.shape[1]
    total = n_z * count
    plane = [(a, b) for a in range(n_row) for b in range(n_y)]
    n_plane = len(plane)
    n_pieces = n_core * n_plane

    def over_plane(value, where):
        return xor_permute(value, ("row", "y"), where)

    def over_z(value, offset):
        return xor_permute(value, ("z",), (offset,))

    def over_core(value):
        return xor_permute(value, ("core",), (1,))

    packed = jax.ShapeDtypeStruct((count + PAD_ROWS, 2 * width), BF16)
    qg, kv = pl.pallas_call(
        functools.partial(pack_kernel, axes),
        out_shape=(packed, packed),
        in_specs=[VMEM] * 6 + [SMEM],
        out_specs=(VMEM, VMEM),
        scratch_shapes=[
            pltpu.VMEM((2 * width, width), F32),
            pltpu.VMEM((PAD_ROWS, 2 * width), F32),
        ],
        compiler_params=params(8 * MIB),
        name="pack",
    )(queries, keys, values, forward_out, out_grad, token_pos.reshape(-1, count), block_sample)

    kv_near = [kv] + [over_plane(kv, where) for where in plane[1:]]
    qg_all = [qg] + [over_z(qg, offset) for offset in range(1, n_z)]
    kv_all = kv_near + [over_core(piece) for piece in kv_near]
    if n_pieces <= 8:
        kv_all = [piece[None] for piece in kv_all]
    else:
        kv_all = [jnp.stack(kv_all)]

    blk = model_width // (n_z * n_y * n_core * n_row)
    row_id, y_id = lax.axis_index("row"), lax.axis_index("y")
    split_input = layer_input.reshape(count, n_z, n_y, n_core, n_row, blk)
    split_input = split_input.transpose(4, 2, 0, 3, 1, 5).reshape(n_plane, count, -1)
    x_send = [
        lax.dynamic_index_in_dim(split_input, (row_id ^ a) * n_y + (y_id ^ b), 0, False)
        for a, b in plane
    ]
    x_all = [x_send[0]] + [over_plane(x, where) for x, where in zip(x_send[1:], plane[1:])]

    mass_rows = 3 * total // LANES
    tail_rows = -(-mass_rows // PAD_ROWS) * PAD_ROWS
    big = jax.ShapeDtypeStruct((n_pieces, count, total), BF16)
    w, u, stat, own_part, *send = pl.pallas_call(
        functools.partial(forward_kernel, count, width, n_z, len(kv_all)),
        out_shape=[
            big,
            big,
            jax.ShapeDtypeStruct((8, total), F32),
            jax.ShapeDtypeStruct((count, width), F32),
        ]
        + [jax.ShapeDtypeStruct((count + tail_rows, width), BF16)] * (n_z - 1),
        in_specs=[VMEM] * (n_z + len(kv_all)),
        out_specs=[VMEM] * (4 + n_z - 1),
        scratch_shapes=[
            pltpu.VMEM((total, width), BF16),
            pltpu.VMEM((total, width), BF16),
            pltpu.VMEM((n_pieces, count, width), BF16),
            pltpu.VMEM((8, total), F32),
        ],
        compiler_params=params(16 * MIB if n_pieces <= 8 else 56 * MIB),
        name="forward",
    )(*qg_all, *kv_all)
    got = [over_z(piece, offset) for offset, piece in enumerate(send, 1)]

    mine, other, query_grad = pl.pallas_call(
        functools.partial(backward_kernel, count, width, n_z),
        out_shape=[
            jax.ShapeDtypeStruct((n_pieces // 2, count, 2 * width), F32),
            jax.ShapeDtypeStruct((n_pieces // 2, count, 2 * width), BF16),
            jax.ShapeDtypeStruct((count, width), BF16),
        ],
        in_specs=[VMEM] * (4 + n_z + n_z - 1),
        out_specs=[VMEM] * 3,
        scratch_shapes=[pltpu.VMEM((total, width), BF16), pltpu.VMEM((total, width), BF16)],
        compiler_params=params(16 * MIB if n_pieces <= 8 else 56 * MIB),
        name="backward",
    )(w, u, stat, own_part, *qg_all, *got)

    both = mine + over_core(other).astype(F32)
    kv_sum = both[0]
    for index, where in enumerate(plane[1:], 1):
        kv_sum = kv_sum + over_plane(both[index].astype(BF16), where).astype(F32)
    kv_grad = kv_sum.astype(BF16)
    all_grads = jnp.concatenate([query_grad, kv_grad], axis=1)
    g_all = [all_grads] + [over_plane(all_grads, where) for where in plane[1:]]

    block = (n_z, blk, 3 * width)
    mine, other = pl.pallas_call(
        functools.partial(weight_kernel, n_plane),
        out_shape=[jax.ShapeDtypeStruct(block, F32), jax.ShapeDtypeStruct(block, BF16)],
        in_specs=[VMEM] * (2 * n_plane),
        out_specs=[VMEM] * 2,
        scratch_shapes=[pltpu.VMEM((n_core,) + block, F32)],
        compiler_params=params(24 * MIB),
        name="weights",
    )(*x_all, *g_all)
    both = mine + over_core(other).astype(F32)
    piece = both[0]
    for offset in range(1, n_z):
        piece = piece + over_z(both[offset].astype(BF16), offset).astype(F32)
    low = piece.astype(BF16)
    parts = [piece] + [xor_permute(low, ("row",), (a,)).astype(F32) for a in range(1, n_row)]
    stacked = jnp.stack(parts)
    stacked = stacked[row_id ^ jnp.arange(n_row)]
    weight_grad = stacked.reshape(n_row * blk, 3 * width)
    return query_grad, kv_grad[:, :width], kv_grad[:, width:], weight_grad


def solution(mesh):
    n_row, n_col = mesh.shape["row"], mesh.shape["col"]
    n_core = 2
    n_z = 1 << ((n_col.bit_length() - 1) // 2)
    n_y = n_col // (n_core * n_z)
    axes = (("row", n_row), ("z", n_z), ("y", n_y), ("core", n_core))
    split = Mesh(
        mesh.devices.reshape(tuple(size for _, size in axes)), tuple(name for name, _ in axes)
    )
    tokens = P(("row", "z", "y", "core"), None)
    return jax.shard_map(
        functools.partial(local, axes),
        mesh=split,
        in_specs=(tokens,) * 6 + (P(), P()),
        out_specs=(tokens, tokens, tokens, P(("z", "y", "core"), None)),
        check_vma=False,
    )
```

```python
import functools
import math

import jax
import jax.numpy as jnp
from jax import lax
from jax.experimental import pallas as pl
from jax.experimental.pallas import tpu as pltpu
from jax.sharding import Mesh
from jax.sharding import PartitionSpec as P

BLK = 128
LANES = 128
PAD_ROWS = 16
NEG_FILL = -1e30
LOG2E = math.log2(math.e)
MIB = 1 << 20
F32 = jnp.float32
BF16 = jnp.bfloat16
VMEM = pl.BlockSpec(memory_space=pltpu.VMEM)
HBM = pl.BlockSpec(memory_space=pltpu.HBM)


def dot_nt(left, right, precision=None):
    return lax.dot_general(
        left, right, (((1,), (1,)), ((), ())), preferred_element_type=F32, precision=precision
    )


def dot_tn(left, right):
    return lax.dot_general(left, right, (((0,), (0,)), ((), ())), preferred_element_type=F32)


def params(nbytes):
    return pltpu.CompilerParams(vmem_limit_bytes=nbytes)


def split_three(values):
    high = values.astype(BF16).astype(F32)
    rest = values - high
    middle = rest.astype(BF16).astype(F32)
    return high, middle, rest - middle


def pack_kernel(
    axes, q_hbm, k_hbm, v_hbm, o_hbm, g_hbm, x_hbm, pos_hbm, ids_hbm, qg_ref, kv_ref, x_ref, *scratch
):
    outs, prod, extra, pos, ids, sems = scratch
    count, width = outs.shape
    copies = [
        pltpu.make_async_copy(source, target, sems.at[place])
        for place, (source, target) in enumerate(
            (
                (pos_hbm, pos),
                (ids_hbm, ids),
                (g_hbm, qg_ref.at[:count, width:]),
                (o_hbm, outs),
                (q_hbm, qg_ref.at[:count, :width]),
                (k_hbm, kv_ref.at[:count, :width]),
                (v_hbm, kv_ref.at[:count, width:]),
                (x_hbm, x_ref),
            )
        )
    ]
    for copy in copies:
        copy.start()
    me = jnp.int32(0)
    for name, size in axes:
        me = me * size + lax.axis_index(name)
    prod[...] = jnp.zeros_like(prod)
    copies[0].wait()
    copies[1].wait()
    lines = min(pos.shape[0], (count + LANES - 2) // LANES + 1)
    first = jnp.minimum(me * count // LANES, pos.shape[0] - lines)
    shift = me * count - first * LANES
    block = jnp.concatenate([pos[pl.ds(first + i, 1), :] for i in range(lines)], axis=1) // BLK

    def add_id(index, found):
        return jnp.where(block == index, ids[index], found)

    found = lax.fori_loop(0, ids.shape[0], add_id, jnp.zeros_like(block), unroll=8)
    found = jnp.broadcast_to(found.astype(F32), (8, lines * LANES))
    found = pltpu.roll(found, lines * LANES - shift, 1)
    copies[2].wait()
    copies[3].wait()
    prod[:count, :] = qg_ref[:count, width:].astype(F32) * outs[...].astype(F32)
    delta = dot_nt(
        jnp.ones((PAD_ROWS, width), F32), prod[...], precision=lax.Precision.HIGHEST
    )
    high, middle, low = split_three(delta)
    row = lax.broadcasted_iota(jnp.int32, delta.shape, 0)
    extra[...] = jnp.where(row == 0, high, jnp.where(row == 1, middle, jnp.where(row == 2, low, 0.0)))
    extra[3:4, :count] = found[0:1, :count]
    tail = extra[...].astype(BF16)
    qg_ref[count:, :] = tail
    kv_ref[count:, :] = tail
    for copy in copies[4:]:
        copy.wait()


def deal_kernel(sizes, x_ref, *refs):
    *out_refs, dealt = refs
    n_row, n_z, n_y, n_core = sizes
    blk = x_ref.shape[1] // (n_row * n_z * n_y * n_core)
    for a in range(n_row):
        for b in range(n_y):
            for core in range(n_core):
                for z in range(n_z):
                    first = (((z * n_y + b) * n_core + core) * n_row + a) * blk
                    dealt[a * n_y + b, core, :, z * blk : (z + 1) * blk] = x_ref[:, first : first + blk]
    me_row, me_y = lax.axis_index("row"), lax.axis_index("y")
    for a in range(n_row):
        for b in range(n_y):
            out_refs[a * n_y + b][...] = dealt[(me_row ^ a) * n_y + (me_y ^ b)]


def assemble_kernel(own_ref, *refs):
    *got_refs, out_ref = refs
    me_row = lax.axis_index("row")
    out_ref[me_row] = own_ref[...]
    for offset, ref in enumerate(got_refs, 1):
        out_ref[me_row ^ offset] = ref[...].astype(F32)


def forward_kernel(count, width, n_q, n_kv, *refs):
    qg_refs, refs = refs[:n_q], refs[n_q:]
    kv_refs, refs = refs[:n_kv], refs[n_kv:]
    w_ref, u_ref, stat_ref, own_ref, refs = *refs[:4], refs[4:]
    send_refs, (queries, grads, keys, rows) = refs[: n_q - 1], refs[n_q - 1 :]
    total = n_q * count
    factor = LOG2E / math.sqrt(width)
    for slot, ref in enumerate(qg_refs):
        queries[slot * count : (slot + 1) * count, :] = ref[:count, :width]
        grads[slot * count : (slot + 1) * count, :] = ref[:count, width:]
        tail = ref[count:, :].astype(F32)
        rows[0:1, slot * count : (slot + 1) * count] = (tail[0:1] + tail[1:2] + tail[2:3])[:, :count]
        rows[1:2, slot * count : (slot + 1) * count] = tail[3:4, :count]
    delta = rows[0:1, :]
    query_ids = rows[1:2, :]

    def over_pieces(body, state):
        base = 0
        for ref in kv_refs:
            depth = ref.shape[0]
            if depth == 1:
                state = body(ref.at[0], base, state)
            else:
                state = lax.fori_loop(
                    0, depth, lambda i, s, ref=ref, base=base: body(ref.at[i], base + i, s), state
                )
            base += depth
        return state

    def scores_of(ref):
        key_ids = jnp.transpose(ref[count:, :].astype(F32))[:count, 3:4]
        scores = dot_nt(ref[:count, :width], queries[...]) * factor
        return jnp.where(key_ids == query_ids, scores, NEG_FILL)

    def fold(values, combine):
        out = values[0:8]
        for start in range(8, count, 8):
            out = combine(out, values[start : start + 8])
        return out

    def peak_step(ref, index, peak):
        return jnp.maximum(peak, fold(scores_of(ref), jnp.maximum))

    peak8 = over_pieces(peak_step, jnp.full((8, total), NEG_FILL, F32))
    peak = jnp.max(peak8, axis=0, keepdims=True)

    def grad_step(ref, index, mass):
        weight = jnp.exp2(scores_of(ref) - peak)
        w_ref[index] = weight.astype(BF16)
        prob_grad = dot_nt(ref[:count, width:], grads[...])
        u_ref[index] = (weight * (prob_grad - delta)).astype(BF16)
        keys[index] = ref[:count, :width]
        return mass + fold(weight, jnp.add)

    mass8 = over_pieces(grad_step, jnp.zeros((8, total), F32))
    mass = jnp.sum(mass8, axis=0, keepdims=True)
    level = peak + jnp.log2(mass)
    stat_ref[...] = jnp.zeros_like(stat_ref)
    stat_ref[0:1, :] = peak
    stat_ref[1:2, :] = level

    n_pieces = keys.shape[0]
    if n_pieces <= 8:
        joined = dot_tn(
            keys[...].reshape(n_pieces * count, width), u_ref[...].reshape(n_pieces * count, total)
        )
    else:
        joined = lax.fori_loop(
            0,
            n_pieces,
            lambda i, s: s + dot_tn(keys[i], u_ref[i]),
            jnp.zeros((width, total), F32),
        )
    query_part = jnp.transpose(joined / mass)
    own_ref[...] = query_part[:count]
    chunks = total // LANES
    parts = split_three(level)
    tail_rows = send_refs[0].shape[0] - count
    lines = [part[:, c * LANES : (c + 1) * LANES] for part in parts for c in range(chunks)]
    row = lax.broadcasted_iota(jnp.int32, (tail_rows, LANES), 0)
    tail = jnp.zeros((tail_rows, LANES), F32)
    for place, line in enumerate(lines):
        tail = jnp.where(row == place, line, tail)
    tail = tail.astype(BF16)
    for slot, ref in enumerate(send_refs, 1):
        ref[:count, :] = query_part[slot * count : (slot + 1) * count].astype(BF16)
        ref[count:, :] = tail


def backward_kernel(count, width, n_q, *refs):
    w_ref, u_ref, stat_ref, own_ref, refs = *refs[:4], refs[4:]
    qg_refs, refs = refs[:n_q], refs[n_q:]
    got_refs, refs = refs[: n_q - 1], refs[n_q - 1 :]
    mine_ref, other_ref, dq_ref, queries, grads = refs
    total = n_q * count
    chunks = total // LANES
    scale = 1.0 / math.sqrt(width)
    stat = jnp.transpose(stat_ref[...])
    peak, level = stat[:, 0:1], stat[:, 1:2]
    levels = [[level[s * count : (s + 1) * count] for s in range(n_q)]]
    for offset, ref in enumerate(got_refs, 1):
        tail = ref[count:, :].astype(F32)
        summed = tail[:chunks] + tail[chunks : 2 * chunks] + tail[2 * chunks : 3 * chunks]
        summed = jnp.concatenate([summed, jnp.zeros((-chunks % 8, LANES), F32)], axis=0)
        across = jnp.transpose(summed)
        column = jnp.concatenate([across[:, c : c + 1] for c in range(chunks)], axis=0)
        levels.append(
            [column[(s ^ offset) * count : ((s ^ offset) + 1) * count] for s in range(n_q)]
        )
    for slot in range(n_q):
        here = [one[slot] for one in levels]
        top = functools.reduce(jnp.maximum, here)
        shares = [jnp.exp2(one - top) for one in here]
        mass = functools.reduce(jnp.add, shares)
        rows = slice(slot * count, (slot + 1) * count)
        share = jnp.exp2(peak[rows] - top) / mass
        queries[rows, :] = (qg_refs[slot][:count, :width].astype(F32) * share).astype(BF16)
        grads[rows, :] = (qg_refs[slot][:count, width:].astype(F32) * share).astype(BF16)
        if slot == 0:
            query_grad = own_ref[...] * shares[0]
            for one, ref in zip(shares[1:], got_refs):
                query_grad = query_grad + ref[:count, :].astype(F32) * one
            dq_ref[...] = (query_grad * (scale / mass)).astype(BF16)

    n_pieces = w_ref.shape[0]
    half = n_pieces // 2

    def emit(first, size, ref, place):
        many = (size * count, total)
        value_part = jnp.dot(
            w_ref[pl.ds(first, size)].reshape(many), grads[...], preferred_element_type=F32
        )
        key_part = jnp.dot(
            u_ref[pl.ds(first, size)].reshape(many), queries[...], preferred_element_type=F32
        )
        shape = (size, count, width)
        ref[pl.ds(place, size), :, :width] = (key_part * scale).reshape(shape).astype(ref.dtype)
        ref[pl.ds(place, size), :, width:] = value_part.reshape(shape).astype(ref.dtype)

    if half <= 4:
        emit(half, half, other_ref, 0)
        emit(0, half, mine_ref, 0)
    else:

        @pl.loop(0, half)
        def _(i):
            emit(half + i, 1, other_ref, i)
            emit(i, 1, mine_ref, i)


def weight_kernel(n_pairs, n_z, *refs):
    x_refs, refs = refs[:n_pairs], refs[n_pairs:]
    g_refs, refs = refs[:n_pairs], refs[n_pairs:]
    out_refs, sums = refs[:n_z], refs[n_z]
    core_id = lax.axis_index("core")
    total = None
    for x_ref, g_ref in zip(x_refs, g_refs):
        part = dot_tn(x_ref[core_id], g_ref[...])
        total = part if total is None else total + part
    sums[...] = total.reshape(sums.shape)
    z_id = lax.axis_index("z")
    for slot, ref in enumerate(out_refs):
        ref[...] = sums[z_id ^ slot].astype(ref.dtype)


def xor_permute(value, names, offsets):
    sizes = [lax.axis_size(name) for name in names]
    pairs = []
    for source in range(math.prod(sizes)):
        rest, digits = source, []
        for size in reversed(sizes):
            digits.append(rest % size)
            rest //= size
        target = 0
        for digit, size, offset in zip(reversed(digits), sizes, offsets):
            target = target * size + (digit ^ offset)
        pairs.append((source, target))
    return lax.ppermute(value, tuple(names), pairs)


def local(axes, layer_input, queries, keys, values, forward_out, out_grad, token_pos, block_sample):
    sizes = dict(axes)
    n_row, n_z, n_y, n_core = (sizes[name] for name in ("row", "z", "y", "core"))
    count, width = queries.shape
    model_width = layer_input.shape[1]
    total = n_z * count
    plane = [(a, b) for a in range(n_row) for b in range(n_y)]
    n_plane = len(plane)
    n_pieces = n_core * n_plane

    def over_plane(value, where):
        return xor_permute(value, ("row", "y"), where)

    def over_z(value, offset):
        return xor_permute(value, ("z",), (offset,))

    def over_core(value):
        return xor_permute(value, ("core",), (1,))

    packed = jax.ShapeDtypeStruct((count + PAD_ROWS, 2 * width), BF16)
    qg, kv, x_here = pl.pallas_call(
        functools.partial(pack_kernel, axes),
        out_shape=(packed, packed, jax.ShapeDtypeStruct(layer_input.shape, BF16)),
        in_specs=[HBM] * 8,
        out_specs=(VMEM, VMEM, VMEM),
        scratch_shapes=[
            pltpu.VMEM((count, width), BF16),
            pltpu.VMEM((2 * width, width), F32),
            pltpu.VMEM((PAD_ROWS, 2 * width), F32),
            pltpu.VMEM((token_pos.shape[0] // LANES, LANES), jnp.int32),
            pltpu.SMEM(block_sample.shape, jnp.int32),
            pltpu.SemaphoreType.DMA((8,)),
        ],
        compiler_params=params(8 * MIB),
        name="pack",
    )(
        *(
            pltpu.with_memory_space_constraint(value, pltpu.HBM)
            for value in (
                queries,
                keys,
                values,
                forward_out,
                out_grad,
                layer_input,
                token_pos.reshape(-1, LANES),
                block_sample,
            )
        )
    )

    blk = model_width // (n_z * n_y * n_core * n_row)
    kv_near = [kv] + [over_plane(kv, where) for where in plane[1:]]
    qg_all = [qg] + [over_z(qg, offset) for offset in range(1, n_z)]
    x_send = pl.pallas_call(
        functools.partial(deal_kernel, (n_row, n_z, n_y, n_core)),
        out_shape=[jax.ShapeDtypeStruct((n_core, count, n_z * blk), BF16)] * n_plane,
        in_specs=[VMEM],
        out_specs=[VMEM] * n_plane,
        scratch_shapes=[pltpu.VMEM((n_plane, n_core, count, n_z * blk), BF16)],
        compiler_params=params(16 * MIB),
        name="deal",
    )(x_here)
    kv_near[1:], x_send = lax.optimization_barrier((kv_near[1:], x_send))
    kv_all = kv_near + [over_core(piece) for piece in kv_near]
    if n_pieces <= 8:
        kv_all = [piece[None] for piece in kv_all]
    else:
        kv_all = [jnp.stack(kv_all)]

    mass_rows = 3 * total // LANES
    tail_rows = -(-mass_rows // PAD_ROWS) * PAD_ROWS
    big = jax.ShapeDtypeStruct((n_pieces, count, total), BF16)
    w, u, stat, own_part, *send = pl.pallas_call(
        functools.partial(forward_kernel, count, width, n_z, len(kv_all)),
        out_shape=[
            big,
            big,
            jax.ShapeDtypeStruct((8, total), F32),
            jax.ShapeDtypeStruct((count, width), F32),
        ]
        + [jax.ShapeDtypeStruct((count + tail_rows, width), BF16)] * (n_z - 1),
        in_specs=[VMEM] * (n_z + len(kv_all)),
        out_specs=[VMEM] * (4 + n_z - 1),
        scratch_shapes=[
            pltpu.VMEM((total, width), BF16),
            pltpu.VMEM((total, width), BF16),
            pltpu.VMEM((n_pieces, count, width), BF16),
            pltpu.VMEM((8, total), F32),
        ],
        compiler_params=params(16 * MIB if n_pieces <= 8 else 56 * MIB),
        name="forward",
    )(*qg_all, *kv_all)
    got = [over_z(piece, offset) for offset, piece in enumerate(send, 1)]
    x_send, stat = lax.optimization_barrier((x_send, stat))
    x_all = [x_send[0]] + [over_plane(x, where) for x, where in zip(x_send[1:], plane[1:])]
    far = [index for index, (a, b) in enumerate(plane) if a and b]
    near = [index for index, (a, b) in enumerate(plane) if (a or b) and not (a and b)]

    def together(values, indices):
        values, some = lax.optimization_barrier((values, [x_all[index] for index in indices]))
        for index, value in zip(indices, some):
            x_all[index] = value
        return values

    got = together(got, far)

    mine, other, query_grad = pl.pallas_call(
        functools.partial(backward_kernel, count, width, n_z),
        out_shape=[
            jax.ShapeDtypeStruct((n_pieces // 2, count, 2 * width), F32),
            jax.ShapeDtypeStruct((n_pieces // 2, count, 2 * width), BF16),
            jax.ShapeDtypeStruct((count, width), BF16),
        ],
        in_specs=[VMEM] * (4 + n_z + n_z - 1),
        out_specs=[VMEM] * 3,
        scratch_shapes=[pltpu.VMEM((total, width), BF16), pltpu.VMEM((total, width), BF16)],
        compiler_params=params(16 * MIB if n_pieces <= 8 else 56 * MIB),
        cost_estimate=pl.CostEstimate(flops=int(3e10), bytes_accessed=0, transcendentals=0),
        name="backward",
    )(w, u, stat, own_part, *qg_all, *got)

    other = together(other, near)
    both = mine + over_core(other).astype(F32)

    x_pair = [over_core(x) for x in x_all]
    arrived = [
        over_plane(both[index].astype(BF16), where) for index, where in enumerate(plane[1:], 1)
    ]
    kv_sum = both[0]
    for part in arrived:
        kv_sum = kv_sum + part.astype(F32)
    kv_grad = kv_sum.astype(BF16)
    all_grads = jnp.concatenate([query_grad, kv_grad], axis=1)
    g_all = [all_grads] + [over_plane(all_grads, where) for where in plane[1:]]
    g_all = g_all + [over_core(g) for g in g_all]
    x_all = x_all + x_pair
    mine, *send = pl.pallas_call(
        functools.partial(weight_kernel, len(x_all), n_z),
        out_shape=[jax.ShapeDtypeStruct((blk, 3 * width), F32)]
        + [jax.ShapeDtypeStruct((blk, 3 * width), BF16)] * (n_z - 1),
        in_specs=[VMEM] * (2 * len(x_all)),
        out_specs=[VMEM] * n_z,
        scratch_shapes=[pltpu.VMEM((n_z, blk, 3 * width), F32)],
        compiler_params=params(24 * MIB),
        name="weights",
    )(*x_all, *g_all)
    both = [mine] + send
    piece = both[0]
    for offset in range(1, n_z):
        piece = piece + over_z(both[offset], offset).astype(F32)
    low = piece.astype(BF16)
    parts = [piece] + [xor_permute(low, ("row",), (a,)) for a in range(1, n_row)]
    weight_grad = pl.pallas_call(
        assemble_kernel,
        out_shape=jax.ShapeDtypeStruct((n_row, blk, 3 * width), F32),
        in_specs=[VMEM] * n_row,
        out_specs=VMEM,
        compiler_params=params(8 * MIB),
        name="assemble",
    )(*parts).reshape(n_row * blk, 3 * width)
    return query_grad, kv_grad[:, :width], kv_grad[:, width:], weight_grad


def solution(mesh):
    n_row, n_col = mesh.shape["row"], mesh.shape["col"]
    n_core = 2
    n_z = 1 << ((n_col.bit_length() - 1) // 2)
    n_y = n_col // (n_core * n_z)
    axes = (("row", n_row), ("z", n_z), ("y", n_y), ("core", n_core))
    split = Mesh(
        mesh.devices.reshape(tuple(size for _, size in axes)), tuple(name for name, _ in axes)
    )
    tokens = P(("row", "z", "y", "core"), None)
    return jax.shard_map(
        functools.partial(local, axes),
        mesh=split,
        in_specs=(tokens,) * 6 + (P(), P()),
        out_specs=(tokens, tokens, tokens, P(("z", "y", "core"), None)),
        check_vma=False,
    )
```

```python
import functools
import math

import jax
import jax.numpy as jnp
from jax import lax
from jax.experimental import pallas as pl
from jax.experimental.pallas import tpu as pltpu
from jax.sharding import Mesh
from jax.sharding import PartitionSpec as P

BLK = 128
LANES = 128
PAD_ROWS = 16
NEG_FILL = -1e30
LOG2E = math.log2(math.e)
MIB = 1 << 20
F32 = jnp.float32
BF16 = jnp.bfloat16
VMEM = pl.BlockSpec(memory_space=pltpu.VMEM)
HBM = pl.BlockSpec(memory_space=pltpu.HBM)


def plane_places(plane, n_y):
    row_id, y_id = lax.axis_index("row"), lax.axis_index("y")
    return [(row_id ^ a) * n_y + (y_id ^ b) for a, b in plane]


def dot_nt(left, right, precision=None):
    return lax.dot_general(
        left, right, (((1,), (1,)), ((), ())), preferred_element_type=F32, precision=precision
    )


def dot_tn(left, right):
    return lax.dot_general(left, right, (((0,), (0,)), ((), ())), preferred_element_type=F32)


def params(nbytes):
    return pltpu.CompilerParams(vmem_limit_bytes=nbytes)


def split_three(values):
    high = values.astype(BF16).astype(F32)
    rest = values - high
    middle = rest.astype(BF16).astype(F32)
    return high, middle, rest - middle


def pack_kernel(
    axes, q_hbm, k_hbm, v_hbm, o_hbm, g_hbm, x_hbm, pos_hbm, ids_hbm, qg_ref, kv_ref, x_ref, *scratch
):
    outs, prod, extra, pos, ids, sems = scratch
    count, width = outs.shape
    copies = [
        pltpu.make_async_copy(source, target, sems.at[place])
        for place, (source, target) in enumerate(
            (
                (pos_hbm, pos),
                (ids_hbm, ids),
                (g_hbm, qg_ref.at[:count, width:]),
                (o_hbm, outs),
                (q_hbm, qg_ref.at[:count, :width]),
                (k_hbm, kv_ref.at[:count, :width]),
                (v_hbm, kv_ref.at[:count, width:]),
                (x_hbm, x_ref),
            )
        )
    ]
    for copy in copies:
        copy.start()
    me = jnp.int32(0)
    for name, size in axes:
        me = me * size + lax.axis_index(name)
    prod[...] = jnp.zeros_like(prod)
    copies[0].wait()
    copies[1].wait()
    lines = min(pos.shape[0], (count + LANES - 2) // LANES + 1)
    first = jnp.minimum(me * count // LANES, pos.shape[0] - lines)
    shift = me * count - first * LANES
    block = jnp.concatenate([pos[pl.ds(first + i, 1), :] for i in range(lines)], axis=1) // BLK

    def add_id(index, found):
        return jnp.where(block == index, ids[index], found)

    found = lax.fori_loop(0, ids.shape[0], add_id, jnp.zeros_like(block), unroll=8)
    found = jnp.broadcast_to(found.astype(F32), (8, lines * LANES))
    found = pltpu.roll(found, lines * LANES - shift, 1)
    copies[2].wait()
    copies[3].wait()
    prod[:count, :] = qg_ref[:count, width:].astype(F32) * outs[...].astype(F32)
    delta = dot_nt(
        jnp.ones((PAD_ROWS, width), F32), prod[...], precision=lax.Precision.HIGHEST
    )
    high, middle, low = split_three(delta)
    row = lax.broadcasted_iota(jnp.int32, delta.shape, 0)
    extra[...] = jnp.where(row == 0, high, jnp.where(row == 1, middle, jnp.where(row == 2, low, 0.0)))
    extra[3:4, :count] = found[0:1, :count]
    tail = extra[...].astype(BF16)
    qg_ref[count:, :] = tail
    kv_ref[count:, :] = tail
    for copy in copies[4:]:
        copy.wait()


def deal_kernel(sizes, x_ref, *refs):
    *out_refs, dealt = refs
    n_row, n_z, n_y, n_core = sizes
    blk = x_ref.shape[1] // (n_row * n_z * n_y * n_core)
    for a in range(n_row):
        for b in range(n_y):
            for core in range(n_core):
                for z in range(n_z):
                    first = (((z * n_y + b) * n_core + core) * n_row + a) * blk
                    dealt[a * n_y + b, core, :, z * blk : (z + 1) * blk] = x_ref[:, first : first + blk]
    me_row, me_y = lax.axis_index("row"), lax.axis_index("y")
    for a in range(n_row):
        for b in range(n_y):
            out_refs[a * n_y + b][...] = dealt[(me_row ^ a) * n_y + (me_y ^ b)]


def assemble_kernel(own_ref, *refs):
    *got_refs, out_ref = refs
    me_row = lax.axis_index("row")
    out_ref[me_row] = own_ref[...]
    for offset, ref in enumerate(got_refs, 1):
        out_ref[me_row ^ offset] = ref[...].astype(F32)


def lines_kernel(count, width, n_q, *refs):
    qg_refs, (queries, grads, rows) = refs[:n_q], refs[n_q:]
    for slot, ref in enumerate(qg_refs):
        where = slice(slot * count, (slot + 1) * count)
        queries[where, :] = ref[:count, :width]
        grads[where, :] = ref[:count, width:]
        tail = ref[count:, :].astype(F32)
        rows[0:1, where] = (tail[0:1] + tail[1:2] + tail[2:3])[:, :count]
        rows[1:2, where] = tail[3:4, :count]


def forward_kernel(count, width, n_q, n_kv, *refs):
    queries, grads, rows, refs = *refs[:3], refs[3:]
    kv_refs, refs = refs[:n_kv], refs[n_kv:]
    w_ref, u_ref, stat_ref, own_ref, refs = *refs[:4], refs[4:]
    send_refs, keys = refs[: n_q - 1], refs[n_q - 1]
    total = n_q * count
    factor = LOG2E / math.sqrt(width)
    delta = rows[0:1, :]
    query_ids = rows[1:2, :]

    def over_pieces(body, state):
        base = 0
        for ref in kv_refs:
            depth = ref.shape[0]
            if depth <= 4:
                for i in range(depth):
                    state = body(ref.at[i], base + i, state)
            else:
                state = lax.fori_loop(
                    0, depth, lambda i, s, ref=ref, base=base: body(ref.at[i], base + i, s), state
                )
            base += depth
        return state

    def scores_of(ref):
        key_ids = jnp.transpose(ref[count:, :].astype(F32))[:count, 3:4]
        scores = dot_nt(ref[:count, :width], queries[...]) * factor
        return jnp.where(key_ids == query_ids, scores, NEG_FILL)

    def fold(values, combine):
        out = values[0:8]
        for start in range(8, count, 8):
            out = combine(out, values[start : start + 8])
        return out

    def peak_step(ref, index, peak):
        return jnp.maximum(peak, fold(scores_of(ref), jnp.maximum))

    peak8 = over_pieces(peak_step, jnp.full((8, total), NEG_FILL, F32))
    peak = jnp.max(peak8, axis=0, keepdims=True)

    def grad_step(ref, index, mass):
        weight = jnp.exp2(scores_of(ref) - peak)
        w_ref[index] = weight.astype(BF16)
        prob_grad = dot_nt(ref[:count, width:], grads[...])
        u_ref[index] = (weight * (prob_grad - delta)).astype(BF16)
        keys[index] = ref[:count, :width]
        return mass + fold(weight, jnp.add)

    mass8 = over_pieces(grad_step, jnp.zeros((8, total), F32))
    mass = jnp.sum(mass8, axis=0, keepdims=True)
    level = peak + jnp.log2(mass)
    stat_ref[...] = jnp.zeros_like(stat_ref)
    stat_ref[0:1, :] = peak
    stat_ref[1:2, :] = level

    n_pieces = keys.shape[0]
    if n_pieces <= 8:
        joined = dot_tn(
            keys[...].reshape(n_pieces * count, width), u_ref[...].reshape(n_pieces * count, total)
        )
    else:
        joined = lax.fori_loop(
            0,
            n_pieces,
            lambda i, s: s + dot_tn(keys[i], u_ref[i]),
            jnp.zeros((width, total), F32),
        )
    query_part = jnp.transpose(joined / mass)
    own_ref[...] = query_part[:count]
    chunks = total // LANES
    parts = split_three(level)
    tail_rows = send_refs[0].shape[0] - count
    step = tail_rows // 4
    row = lax.broadcasted_iota(jnp.int32, (tail_rows, LANES), 0)
    tail = jnp.zeros((tail_rows, LANES), F32)
    for index, part in enumerate(parts):
        for chunk in range(chunks):
            line = part[:, chunk * LANES : (chunk + 1) * LANES]
            tail = jnp.where(row == index * step + chunk, line, tail)
    tail = tail.astype(BF16)
    for slot, ref in enumerate(send_refs, 1):
        ref[:count, :] = query_part[slot * count : (slot + 1) * count].astype(BF16)
        ref[count:, :] = tail


def backward_kernel(count, width, n_q, plane, n_y, *refs):
    w_ref, u_ref, stat_ref, own_ref, all_queries, all_grads, refs = *refs[:6], refs[6:]
    got_refs, refs = refs[: n_q - 1], refs[n_q - 1 :]
    mine_k_ref, mine_v_ref, other_k_ref, other_v_ref, dq_ref, queries, grads = refs
    total = n_q * count
    chunks = total // LANES
    scale = 1.0 / math.sqrt(width)
    stat = jnp.transpose(stat_ref[...])
    peak, level = stat[:, 0:1], stat[:, 1:2]
    levels = [[level[s * count : (s + 1) * count] for s in range(n_q)]]
    for offset, ref in enumerate(got_refs, 1):
        tail = ref[count:, :].astype(F32)
        step = tail.shape[0] // 4
        across = jnp.transpose(tail[:step] + tail[step : 2 * step] + tail[2 * step : 3 * step])
        column = jnp.concatenate([across[:, c : c + 1] for c in range(chunks)], axis=0)
        levels.append(
            [column[(s ^ offset) * count : ((s ^ offset) + 1) * count] for s in range(n_q)]
        )
    for slot in range(n_q):
        here = [one[slot] for one in levels]
        top = functools.reduce(jnp.maximum, here)
        shares = [jnp.exp2(one - top) for one in here]
        mass = functools.reduce(jnp.add, shares)
        rows = slice(slot * count, (slot + 1) * count)
        share = jnp.exp2(peak[rows] - top) / mass
        queries[rows, :] = (all_queries[rows, :].astype(F32) * share).astype(BF16)
        grads[rows, :] = (all_grads[rows, :].astype(F32) * share).astype(BF16)
        if slot == 0:
            query_grad = own_ref[...] * shares[0]
            for one, ref in zip(shares[1:], got_refs):
                query_grad = query_grad + ref[:count, :].astype(F32) * one
            dq_ref[...] = query_grad * (scale / mass)

    n_pieces = w_ref.shape[0]
    half = n_pieces // 2

    def emit(first, size, places, key_ref, value_ref):
        many = (size * count, total)
        shape = (size, count, width)
        value_part = jnp.dot(
            w_ref[pl.ds(first, size)].reshape(many), grads[...], preferred_element_type=F32
        ).reshape(shape)
        key_part = jnp.dot(
            u_ref[pl.ds(first, size)].reshape(many), queries[...], preferred_element_type=F32
        ).reshape(shape)
        for step, place in enumerate(places):
            key_ref[place] = (key_part[step] * scale).astype(key_ref.dtype)
            value_ref[place] = value_part[step].astype(value_ref.dtype)

    places = plane_places(plane, n_y)
    if half <= 4:
        emit(half, half, places, other_k_ref, other_v_ref)
        emit(0, half, places, mine_k_ref, mine_v_ref)
    else:
        for i, place in enumerate(places):
            emit(half + i, 1, [place], other_k_ref, other_v_ref)
            emit(i, 1, [place], mine_k_ref, mine_v_ref)


def weight_kernel(plane, n_y, n_core, n_z, *refs):
    n_plane = len(plane)
    n_pairs = n_core * n_plane
    x_refs, refs = refs[:n_pairs], refs[n_pairs:]
    g_refs, refs = refs[: 3 * n_core], refs[3 * n_core :]
    out_refs, (inputs, grads, sums) = refs[:n_z], refs[n_z:]
    count, width = g_refs[1].shape[1:]
    places = plane_places(plane, n_y)
    core_id, z_id = lax.axis_index("core"), lax.axis_index("z")
    for core in range(n_core):
        query_ref, key_ref, value_ref = g_refs[3 * core : 3 * core + 3]
        for slot, place in enumerate(places):
            index = core * n_plane + slot
            rows = slice(index * count, (index + 1) * count)
            inputs[rows, :] = x_refs[index][core_id]
            grads[rows, :width] = query_ref[slot * count : (slot + 1) * count, :]
            grads[rows, width : 2 * width] = key_ref[place]
            grads[rows, 2 * width :] = value_ref[place]
    sums[...] = dot_tn(inputs[...], grads[...]).reshape(sums.shape)
    for slot, ref in enumerate(out_refs):
        ref[...] = sums[z_id ^ slot].astype(ref.dtype)


def xor_permute(value, names, offsets):
    sizes = [lax.axis_size(name) for name in names]
    pairs = []
    for source in range(math.prod(sizes)):
        rest, digits = source, []
        for size in reversed(sizes):
            digits.append(rest % size)
            rest //= size
        target = 0
        for digit, size, offset in zip(reversed(digits), sizes, offsets):
            target = target * size + (digit ^ offset)
        pairs.append((source, target))
    return lax.ppermute(value, tuple(names), pairs)


def local(axes, layer_input, queries, keys, values, forward_out, out_grad, token_pos, block_sample):
    sizes = dict(axes)
    n_row, n_z, n_y, n_core = (sizes[name] for name in ("row", "z", "y", "core"))
    count, width = queries.shape
    model_width = layer_input.shape[1]
    total = n_z * count
    plane = [(a, b) for a in range(n_row) for b in range(n_y)]
    n_plane = len(plane)
    n_pieces = n_core * n_plane

    def over_plane(value, where):
        return xor_permute(value, ("row", "y"), where)

    def over_z(value, offset):
        return xor_permute(value, ("z",), (offset,))

    def over_core(value):
        return xor_permute(value, ("core",), (1,))

    packed = jax.ShapeDtypeStruct((count + PAD_ROWS, 2 * width), BF16)
    qg, kv, x_here = pl.pallas_call(
        functools.partial(pack_kernel, axes),
        out_shape=(packed, packed, jax.ShapeDtypeStruct(layer_input.shape, BF16)),
        in_specs=[HBM] * 8,
        out_specs=(VMEM, VMEM, VMEM),
        scratch_shapes=[
            pltpu.VMEM((count, width), BF16),
            pltpu.VMEM((2 * width, width), F32),
            pltpu.VMEM((PAD_ROWS, 2 * width), F32),
            pltpu.VMEM((token_pos.shape[0] // LANES, LANES), jnp.int32),
            pltpu.SMEM(block_sample.shape, jnp.int32),
            pltpu.SemaphoreType.DMA((8,)),
        ],
        compiler_params=params(8 * MIB),
        name="pack",
    )(
        *(
            pltpu.with_memory_space_constraint(value, pltpu.HBM)
            for value in (
                queries,
                keys,
                values,
                forward_out,
                out_grad,
                layer_input,
                token_pos.reshape(-1, LANES),
                block_sample,
            )
        )
    )

    blk = model_width // (n_z * n_y * n_core * n_row)
    kv_near = [kv] + [over_plane(kv, where) for where in plane[1:]]
    qg_all = [qg] + [over_z(qg, offset) for offset in range(1, n_z)]
    x_send = pl.pallas_call(
        functools.partial(deal_kernel, (n_row, n_z, n_y, n_core)),
        out_shape=[jax.ShapeDtypeStruct((n_core, count, n_z * blk), BF16)] * n_plane,
        in_specs=[VMEM],
        out_specs=[VMEM] * n_plane,
        scratch_shapes=[pltpu.VMEM((n_plane, n_core, count, n_z * blk), BF16)],
        compiler_params=params(16 * MIB),
        name="deal",
    )(x_here)
    stacked = jnp.stack(kv_near)
    kv_all = [piece[None] for piece in kv_near] if n_pieces <= 8 else [stacked]
    kv_all = kv_all + [over_core(stacked)]

    tail_rows = 4 * -(-total // (8 * LANES)) * 8
    big = jax.ShapeDtypeStruct((n_pieces, count, total), BF16)
    lines = pl.pallas_call(
        functools.partial(lines_kernel, count, width, n_z),
        out_shape=[
            jax.ShapeDtypeStruct((total, width), BF16),
            jax.ShapeDtypeStruct((total, width), BF16),
            jax.ShapeDtypeStruct((8, total), F32),
        ],
        in_specs=[VMEM] * n_z,
        out_specs=[VMEM] * 3,
        compiler_params=params(8 * MIB),
        cost_estimate=pl.CostEstimate(flops=int(5e9), bytes_accessed=0, transcendentals=0),
        name="lines",
    )(*qg_all)
    w, u, stat, own_part, *send = pl.pallas_call(
        functools.partial(forward_kernel, count, width, n_z, len(kv_all)),
        out_shape=[
            big,
            big,
            jax.ShapeDtypeStruct((8, total), F32),
            jax.ShapeDtypeStruct((count, width), F32),
        ]
        + [jax.ShapeDtypeStruct((count + tail_rows, width), BF16)] * (n_z - 1),
        in_specs=[VMEM] * (3 + len(kv_all)),
        out_specs=[VMEM] * (4 + n_z - 1),
        scratch_shapes=[pltpu.VMEM((n_pieces, count, width), BF16)],
        compiler_params=params(16 * MIB if n_pieces <= 8 else 56 * MIB),
        cost_estimate=pl.CostEstimate(flops=int(3e10), bytes_accessed=0, transcendentals=0),
        name="forward",
    )(*lines, *kv_all)
    got = [over_z(piece, offset) for offset, piece in enumerate(send, 1)]
    x_all = [x_send[0]] + [over_plane(x, where) for x, where in zip(x_send[1:], plane[1:])]
    far = [index for index, (a, b) in enumerate(plane) if a and b]
    near = [index for index, (a, b) in enumerate(plane) if (a or b) and not (a and b)]

    def together(values, indices):
        values, some = lax.optimization_barrier((values, [x_all[index] for index in indices]))
        for index, value in zip(indices, some):
            x_all[index] = value
        return values

    got = together(got, far + near)

    half = (n_plane, count, width)
    mine_k, mine_v, other_k, other_v, query_sum = pl.pallas_call(
        functools.partial(backward_kernel, count, width, n_z, plane, n_y),
        out_shape=[jax.ShapeDtypeStruct(half, F32 if n_pieces <= 8 else BF16)] * 2
        + [jax.ShapeDtypeStruct(half, BF16)] * 2
        + [jax.ShapeDtypeStruct((count, width), F32)],
        in_specs=[VMEM] * (6 + n_z - 1),
        out_specs=[VMEM] * 5,
        scratch_shapes=[pltpu.VMEM((total, width), BF16), pltpu.VMEM((total, width), BF16)],
        compiler_params=params(16 * MIB if n_pieces <= 8 else 56 * MIB),
        cost_estimate=pl.CostEstimate(flops=int(3e10), bytes_accessed=0, transcendentals=0),
        name="backward",
    )(w, u, stat, own_part, *lines[:2], *got)
    query_grad = query_sum.astype(BF16)

    key_sum = mine_k.astype(F32) + over_core(other_k).astype(F32)
    value_sum = mine_v.astype(F32) + over_core(other_v).astype(F32)
    x_pair = [over_core(x) for x in x_all]
    row_bits = [(1 << bit, 0) for bit in range(n_row.bit_length() - 1)]
    y_bits = [(0, 1 << bit) for bit in range(n_y.bit_length() - 1)]
    query_pieces = {(0, 0): query_grad}
    for key_hop, value_hop in zip(row_bits + y_bits, y_bits + row_bits):
        offsets = list(query_pieces)
        sent = [key_sum.astype(BF16).reshape(n_plane * count, width)]
        sent = jnp.concatenate(sent + [query_pieces[offset] for offset in offsets])
        sent, value_sent = lax.optimization_barrier((sent, value_sum.astype(BF16)))
        key_got, value_got = lax.optimization_barrier(
            (over_plane(sent, key_hop), over_plane(value_sent, value_hop))
        )
        key_sum = key_sum + key_got[: n_plane * count].reshape(half).astype(F32)
        value_sum = value_sum + value_got.astype(F32)
        for index, (a, b) in enumerate(offsets, n_plane):
            piece = key_got[index * count : (index + 1) * count]
            query_pieces[a ^ key_hop[0], b ^ key_hop[1]] = piece
    place = plane_places(plane, n_y)[0]
    key_low, value_low = key_sum.astype(BF16), value_sum.astype(BF16)
    key_grad = lax.dynamic_index_in_dim(key_low, place, 0, False)
    value_grad = lax.dynamic_index_in_dim(value_low, place, 0, False)
    g_near = [jnp.concatenate([query_pieces[where] for where in plane]), key_low, value_low]
    g_all = g_near + [over_core(g) for g in g_near]

    x_all = x_all + x_pair
    rows = n_pieces * count
    mine, *send = pl.pallas_call(
        functools.partial(weight_kernel, plane, n_y, n_core, n_z),
        out_shape=[jax.ShapeDtypeStruct((blk, 3 * width), F32)]
        + [jax.ShapeDtypeStruct((blk, 3 * width), BF16)] * (n_z - 1),
        in_specs=[VMEM] * (n_pieces + 3 * n_core),
        out_specs=[VMEM] * n_z,
        scratch_shapes=[
            pltpu.VMEM((rows, n_z * blk), BF16),
            pltpu.VMEM((rows, 3 * width), BF16),
            pltpu.VMEM((n_z, blk, 3 * width), F32),
        ],
        compiler_params=params(24 * MIB if n_pieces <= 8 else 56 * MIB),
        name="weights",
    )(*x_all, *g_all)
    both = [mine] + send
    piece = both[0]
    for offset in range(1, n_z):
        piece = piece + over_z(both[offset], offset).astype(F32)
    low = piece.astype(BF16)
    parts = [piece] + [xor_permute(low, ("row",), (a,)) for a in range(1, n_row)]
    weight_grad = pl.pallas_call(
        assemble_kernel,
        out_shape=jax.ShapeDtypeStruct((n_row, blk, 3 * width), F32),
        in_specs=[VMEM] * n_row,
        out_specs=VMEM,
        compiler_params=params(8 * MIB),
        name="assemble",
    )(*parts).reshape(n_row * blk, 3 * width)
    return query_grad, key_grad, value_grad, weight_grad


def solution(mesh):
    n_row, n_col = mesh.shape["row"], mesh.shape["col"]
    n_core = 2
    n_z = 1 << ((n_col.bit_length() - 1) // 2)
    n_y = n_col // (n_core * n_z)
    axes = (("row", n_row), ("z", n_z), ("y", n_y), ("core", n_core))
    split = Mesh(
        mesh.devices.reshape(tuple(size for _, size in axes)), tuple(name for name, _ in axes)
    )
    tokens = P(("row", "z", "y", "core"), None)
    return jax.shard_map(
        functools.partial(local, axes),
        mesh=split,
        in_specs=(tokens,) * 6 + (P(), P()),
        out_specs=(tokens, tokens, tokens, P(("z", "y", "core"), None)),
        check_vma=False,
    )
```

```python
import functools
import math

import jax
import jax.numpy as jnp
from jax import lax
from jax.experimental import pallas as pl
from jax.experimental.pallas import tpu as pltpu
from jax.sharding import Mesh
from jax.sharding import PartitionSpec as P

BLK = 128
LANES = 128
PAD_ROWS = 16
NEG_FILL = -1e30
LOG2E = math.log2(math.e)
MIB = 1 << 20
F32 = jnp.float32
BF16 = jnp.bfloat16
VMEM = pl.BlockSpec(memory_space=pltpu.VMEM)
HBM = pl.BlockSpec(memory_space=pltpu.HBM)


def cut_rows(count):
    return count * 3 // (4 * PAD_ROWS) * PAD_ROWS


def plane_places(plane, n_y):
    row_id, y_id = lax.axis_index("row"), lax.axis_index("y")
    return [(row_id ^ a) * n_y + (y_id ^ b) for a, b in plane]


def dot_nt(left, right, precision=None):
    return lax.dot_general(
        left, right, (((1,), (1,)), ((), ())), preferred_element_type=F32, precision=precision
    )


def dot_tn(left, right):
    return lax.dot_general(left, right, (((0,), (0,)), ((), ())), preferred_element_type=F32)


def params(nbytes):
    return pltpu.CompilerParams(vmem_limit_bytes=nbytes)


def split_three(values):
    high = values.astype(BF16).astype(F32)
    rest = values - high
    middle = rest.astype(BF16).astype(F32)
    return high, middle, rest - middle


def pack_kernel(
    axes, q_hbm, k_hbm, v_hbm, o_hbm, g_hbm, x_hbm, pos_hbm, ids_hbm, qg_ref, kv_ref, x_ref, *scratch
):
    outs, prod, extra, pos, ids, sems = scratch
    count, width = outs.shape
    copies = [
        pltpu.make_async_copy(source, target, sems.at[place])
        for place, (source, target) in enumerate(
            (
                (pos_hbm, pos),
                (ids_hbm, ids),
                (g_hbm, qg_ref.at[:count, width:]),
                (o_hbm, outs),
                (q_hbm, qg_ref.at[:count, :width]),
                (k_hbm, kv_ref.at[:count, :width]),
                (v_hbm, kv_ref.at[:count, width:]),
                (x_hbm, x_ref),
            )
        )
    ]
    for copy in copies:
        copy.start()
    me = jnp.int32(0)
    for name, size in axes:
        me = me * size + lax.axis_index(name)
    prod[...] = jnp.zeros_like(prod)
    copies[0].wait()
    copies[1].wait()
    lines = min(pos.shape[0], (count + LANES - 2) // LANES + 1)
    first = jnp.minimum(me * count // LANES, pos.shape[0] - lines)
    shift = me * count - first * LANES
    block = jnp.concatenate([pos[pl.ds(first + i, 1), :] for i in range(lines)], axis=1) // BLK

    def add_id(index, found):
        return jnp.where(block == index, ids[index], found)

    found = lax.fori_loop(0, ids.shape[0], add_id, jnp.zeros_like(block), unroll=8)
    found = jnp.broadcast_to(found.astype(F32), (8, lines * LANES))
    found = pltpu.roll(found, lines * LANES - shift, 1)
    copies[2].wait()
    copies[3].wait()
    prod[:count, :] = qg_ref[:count, width:].astype(F32) * outs[...].astype(F32)
    delta = dot_nt(
        jnp.ones((PAD_ROWS, width), F32), prod[...], precision=lax.Precision.HIGHEST
    )
    high, middle, low = split_three(delta)
    row = lax.broadcasted_iota(jnp.int32, delta.shape, 0)
    extra[...] = jnp.where(row == 0, high, jnp.where(row == 1, middle, jnp.where(row == 2, low, 0.0)))
    extra[3:4, :count] = found[0:1, :count]
    tail = extra[...].astype(BF16)
    qg_ref[count:, :] = tail
    kv_ref[count:, :] = tail
    for copy in copies[4:]:
        copy.wait()


def deal_kernel(sizes, x_ref, *refs):
    *out_refs, dealt = refs
    n_row, n_z, n_y, n_core = sizes
    blk = x_ref.shape[1] // (n_row * n_z * n_y * n_core)
    for a in range(n_row):
        for b in range(n_y):
            for core in range(n_core):
                for z in range(n_z):
                    first = (((z * n_y + b) * n_core + core) * n_row + a) * blk
                    dealt[a * n_y + b, core, :, z * blk : (z + 1) * blk] = x_ref[:, first : first + blk]
    me_row, me_y = lax.axis_index("row"), lax.axis_index("y")
    for a in range(n_row):
        for b in range(n_y):
            out_refs[a * n_y + b][...] = dealt[(me_row ^ a) * n_y + (me_y ^ b)]


def assemble_kernel(own_ref, *refs):
    *got_refs, out_ref = refs
    me_row = lax.axis_index("row")
    out_ref[me_row] = own_ref[...]
    for offset, ref in enumerate(got_refs, 1):
        out_ref[me_row ^ offset] = ref[...].astype(F32)


def line_rows(slot, count):
    place = lax.axis_index("z") ^ slot
    return pl.ds(pl.multiple_of(place * count, PAD_ROWS), count)


def lines_kernel(count, width, n_q, *refs):
    qg_refs, (queries, grads, rows) = refs[:n_q][::-1], refs[n_q:]
    z_id = lax.axis_index("z")
    for slot, ref in enumerate(qg_refs):
        queries[line_rows(slot, count), :] = ref[:count, :width]
        grads[line_rows(slot, count), :] = ref[:count, width:]
    tails = [ref[count:, :].astype(F32) for ref in qg_refs]
    deltas = [(tail[0:1] + tail[1:2] + tail[2:3])[:, :count] for tail in tails]
    samples = [tail[3:4, :count] for tail in tails]
    for place in range(n_q):
        where = slice(place * count, (place + 1) * count)
        delta, sample = deltas[0], samples[0]
        for slot in range(1, n_q):
            here = (z_id ^ slot) == place
            delta = jnp.where(here, deltas[slot], delta)
            sample = jnp.where(here, samples[slot], sample)
        rows[0:1, where] = delta
        rows[1:2, where] = sample


def forward_kernel(count, width, n_q, n_kv, *refs):
    queries, grads, lines, refs = *refs[:3], refs[3:]
    kv_refs, refs = refs[:n_kv], refs[n_kv:]
    w_ref, u_ref, stat_ref, own_ref, refs = *refs[:4], refs[4:]
    send_refs, (keys, values, samples, scores, slopes, parts) = refs[: n_q - 1], refs[n_q - 1 :]
    total = n_q * count
    factor = LOG2E / math.sqrt(width)
    delta, query_samples = lines[0:1, :], lines[1:2, :]
    n_pieces = w_ref.shape[0]
    block = scores.shape[0]
    n_blocks = n_pieces // block

    def load(ref, index):
        keys[index] = ref[:count, :width]
        values[index] = ref[:count, width:]
        samples[index] = jnp.transpose(ref[count:, :].astype(F32))[:count, :8]

    base = 0
    for ref in kv_refs:
        depth = ref.shape[0]
        if depth <= 4:
            for i in range(depth):
                load(ref.at[i], base + i)
        else:

            @pl.loop(0, depth)
            def _(i, ref=ref, base=base):
                load(ref.at[i], base + i)

        base += depth

    def over_blocks(body, state):
        if n_blocks == 1:
            return body(0, state)
        return lax.fori_loop(0, n_blocks, lambda i, s: body(i * block, s), state)

    def fold(part, combine):
        out = part[0:8]
        for start in range(8, count, 8):
            out = combine(out, part[start : start + 8])
        return out

    def product(left, right, first):
        left = left[pl.ds(first, block)].reshape(block * count, width)
        return dot_nt(left, right[...]).reshape(block, count, total)

    def peak_step(first, peak):
        scores[...] = product(keys, queries, first)
        if n_blocks == 1:
            slopes[...] = product(values, grads, first)
        for piece in range(block):
            live = samples[first + piece][:, 3:4] == query_samples
            masked = jnp.where(live, scores[piece], NEG_FILL)
            scores[piece] = masked
            peak = jnp.maximum(peak, fold(masked, jnp.maximum))
        return peak

    turned = jnp.transpose(keys[:block].reshape(block * count, width))

    peak8 = over_blocks(peak_step, jnp.full((8, total), NEG_FILL, F32))
    peak = jnp.max(peak8, axis=0, keepdims=True)

    def grad_step(first, mass):
        if n_blocks > 1:
            peak_step(first, peak8)
            slopes[...] = product(values, grads, first)
        for piece in range(block):
            weight = jnp.exp2((scores[piece] - peak) * factor)
            w_ref[first + piece] = weight.astype(BF16)
            u_ref[first + piece] = (weight * (slopes[piece] - delta)).astype(BF16)
            mass = mass + fold(weight, jnp.add)
            if n_blocks == 1 and (piece + 1) % 4 == 0:
                rows = 4 * count
                first_row = (piece + 1) * count - rows
                known = u_ref[piece + 1 - 4 : piece + 1].reshape(rows, total)
                left = turned[:, first_row : first_row + rows]
                joins.append(jnp.dot(left, known, preferred_element_type=F32))
        return mass

    joins = []
    mass8 = over_blocks(grad_step, jnp.zeros((8, total), F32))
    mass = jnp.sum(mass8, axis=0, keepdims=True)
    level = peak * factor + jnp.log2(mass)
    stat_ref[...] = jnp.zeros_like(stat_ref)
    stat_ref[0:1, :] = peak * factor
    stat_ref[1:2, :] = level

    def join_step(first, joined):
        rows = block * count
        return joined + dot_tn(
            keys[pl.ds(first, block)].reshape(rows, width),
            u_ref[pl.ds(first, block)].reshape(rows, total),
        )

    if n_blocks == 1:
        joined = functools.reduce(jnp.add, joins)
    else:
        joined = over_blocks(join_step, jnp.zeros((width, total), F32))
    parts[...] = jnp.transpose((joined * (1.0 / mass)).astype(BF16))
    own_ref[...] = parts[line_rows(0, count), :]
    tail_rows = send_refs[0].shape[0] - count
    step = tail_rows // 4
    row = lax.broadcasted_iota(jnp.int32, (tail_rows, LANES), 0)
    tail = jnp.zeros((tail_rows, LANES), F32)
    for index, part in enumerate(split_three(level)):
        for chunk in range(total // LANES):
            line = part[:, chunk * LANES : (chunk + 1) * LANES]
            tail = jnp.where(row == index * step + chunk, line, tail)
    for offset, ref in enumerate(send_refs, 1):
        ref[:count, :] = parts[line_rows(offset, count), :]
        ref[count:, :] = tail.astype(BF16)


def products(w_ref, u_ref, first, size, places, queries, grads, key_ref, value_ref, scale):
    _, count, total = w_ref.shape
    many, shape = (size * count, total), (size, count, key_ref.shape[2])
    value_part = jnp.dot(
        w_ref[pl.ds(first, size)].reshape(many), grads[...], preferred_element_type=F32
    ).reshape(shape)
    key_part = jnp.dot(
        u_ref[pl.ds(first, size)].reshape(many), queries[...], preferred_element_type=F32
    ).reshape(shape)
    for step, place in enumerate(places):
        key_ref[place] = (key_part[step] * scale).astype(key_ref.dtype)
        value_ref[place] = value_part[step].astype(value_ref.dtype)


def away_kernel(count, width, n_q, plane, n_y, *refs):
    w_ref, u_ref, stat_ref, all_queries, all_grads, refs = *refs[:5], refs[5:]
    got_refs, refs = refs[: n_q - 1][::-1], refs[n_q - 1 :]
    other_k_ref, other_v_ref, queries, grads, shares_ref, table = refs
    chunks = n_q * count // LANES
    scale = 1.0 / math.sqrt(width)
    levels = [stat_ref[1:2, :]]
    for ref in got_refs:
        tail = ref[count:, :].astype(F32)
        step = tail.shape[0] // 4
        summed = tail[:step] + tail[step : 2 * step] + tail[2 * step : 3 * step]
        levels.append(jnp.concatenate([summed[c : c + 1] for c in range(chunks)], axis=1))
    top = functools.reduce(jnp.maximum, levels)
    shares = [jnp.exp2(one - top) for one in levels]
    inverse = 1.0 / functools.reduce(jnp.add, shares)
    table[...] = jnp.zeros_like(table)
    table[0:1, :] = jnp.exp2(stat_ref[0:1, :] - top) * inverse
    for index, share in enumerate(shares, 1):
        table[index : index + 1, :] = share * inverse * scale
    columns = jnp.transpose(table[...])
    shares_ref[...] = columns
    queries[...] = (all_queries[...].astype(F32) * columns[:, 0:1]).astype(BF16)
    grads[...] = (all_grads[...].astype(F32) * columns[:, 0:1]).astype(BF16)
    half = w_ref.shape[0] // 2
    places = plane_places(plane, n_y)
    if half <= 4:
        products(
            w_ref, u_ref, half, half, places, queries, grads, other_k_ref, other_v_ref, scale
        )
    else:
        for i, place in enumerate(places):
            products(
                w_ref, u_ref, half + i, 1, [place], queries, grads, other_k_ref, other_v_ref, scale
            )


def query_kernel(own_ref, shares_ref, *refs):
    *got_refs, low_ref, high_ref = refs
    count, _ = own_ref.shape
    own = shares_ref[line_rows(0, count), :]
    query_grad = own_ref[...].astype(F32) * own[:, 1:2]
    for index, ref in enumerate(got_refs, 2):
        query_grad = query_grad + ref[:count, :].astype(F32) * own[:, index : index + 1]
    cut = low_ref.shape[0]
    low_ref[...] = query_grad[:cut].astype(BF16)
    high_ref[...] = query_grad[cut:].astype(BF16)


def home_kernel(plane, n_y, w_ref, u_ref, queries, grads, key_ref, value_ref):
    half = w_ref.shape[0] // 2
    places = plane_places(plane, n_y)
    scale = 1.0 / math.sqrt(queries.shape[1])
    if half <= 4:
        products(w_ref, u_ref, 0, half, places, queries, grads, key_ref, value_ref, scale)
    else:
        for i, place in enumerate(places):
            products(w_ref, u_ref, i, 1, [place], queries, grads, key_ref, value_ref, scale)


def token_product(plane, n_y, x_refs, g_refs, inputs, grads):
    query_ref, key_ref, value_ref = g_refs
    n_plane = len(plane)
    count, width = key_ref.shape[1:]
    cut = cut_rows(count)
    high, rest = n_plane * cut, count - cut
    core_id = lax.axis_index("core")
    for slot, place in enumerate(plane_places(plane, n_y)):
        rows = slice(slot * count, (slot + 1) * count)
        inputs[rows, :] = x_refs[slot][core_id]
        middle = slot * count + cut
        grads[slot * count : middle, :width] = query_ref[slot * cut : (slot + 1) * cut, :]
        grads[middle : (slot + 1) * count, :width] = query_ref[
            high + slot * rest : high + (slot + 1) * rest, :
        ]
        grads[rows, width : 2 * width] = key_ref[place]
        grads[rows, 2 * width :] = value_ref[place]
    return dot_tn(inputs[...], grads[...])


def near_kernel(plane, n_y, *refs):
    x_refs, g_refs = refs[: len(plane)], refs[len(plane) : len(plane) + 3]
    sum_ref, inputs, grads = refs[len(plane) + 3 :]
    sum_ref[...] = token_product(plane, n_y, x_refs, g_refs, inputs, grads)


def far_kernel(plane, n_y, n_z, near_ref, *refs):
    x_refs, g_refs = refs[: len(plane)], refs[len(plane) : len(plane) + 3]
    refs = refs[len(plane) + 3 :]
    out_refs, (inputs, grads, sums) = refs[:n_z], refs[n_z:]
    total = near_ref[...] + token_product(plane, n_y, x_refs, g_refs, inputs, grads)
    sums[...] = total.reshape(sums.shape)
    z_id = lax.axis_index("z")
    for slot, ref in enumerate(out_refs):
        ref[...] = sums[z_id ^ slot].astype(ref.dtype)


def xor_permute(value, names, offsets):
    sizes = [lax.axis_size(name) for name in names]
    pairs = []
    for source in range(math.prod(sizes)):
        rest, digits = source, []
        for size in reversed(sizes):
            digits.append(rest % size)
            rest //= size
        target = 0
        for digit, size, offset in zip(reversed(digits), sizes, offsets):
            target = target * size + (digit ^ offset)
        pairs.append((source, target))
    return lax.ppermute(value, tuple(names), pairs)


def local(axes, layer_input, queries, keys, values, forward_out, out_grad, token_pos, block_sample):
    sizes = dict(axes)
    n_row, n_z, n_y, n_core = (sizes[name] for name in ("row", "z", "y", "core"))
    count, width = queries.shape
    model_width = layer_input.shape[1]
    total = n_z * count
    plane = [(a, b) for a in range(n_row) for b in range(n_y)]
    n_plane = len(plane)
    n_pieces = n_core * n_plane

    def over_plane(value, where):
        return xor_permute(value, ("row", "y"), where)

    def over_z(values):
        far_first = reversed(list(enumerate(values, 1)))
        return [xor_permute(value, ("z",), (offset,)) for offset, value in far_first][::-1]

    def over_core(value):
        return xor_permute(value, ("core",), (1,))

    packed = jax.ShapeDtypeStruct((count + PAD_ROWS, 2 * width), BF16)
    qg, kv, x_here = pl.pallas_call(
        functools.partial(pack_kernel, axes),
        out_shape=(packed, packed, jax.ShapeDtypeStruct(layer_input.shape, BF16)),
        in_specs=[HBM] * 8,
        out_specs=(VMEM, VMEM, VMEM),
        scratch_shapes=[
            pltpu.VMEM((count, width), BF16),
            pltpu.VMEM((2 * width, width), F32),
            pltpu.VMEM((PAD_ROWS, 2 * width), F32),
            pltpu.VMEM((token_pos.shape[0] // LANES, LANES), jnp.int32),
            pltpu.SMEM(block_sample.shape, jnp.int32),
            pltpu.SemaphoreType.DMA((8,)),
        ],
        compiler_params=params(8 * MIB),
        name="pack",
    )(
        *(
            pltpu.with_memory_space_constraint(value, pltpu.HBM)
            for value in (
                queries,
                keys,
                values,
                forward_out,
                out_grad,
                layer_input,
                token_pos.reshape(-1, LANES),
                block_sample,
            )
        )
    )

    blk = model_width // (n_z * n_y * n_core * n_row)
    kv_near = [kv] + [over_plane(kv, where) for where in plane[1:]]
    qg_all = [qg] + over_z([qg] * (n_z - 1))
    x_here, kv_near[1] = lax.optimization_barrier((x_here, kv_near[1]))
    x_send = pl.pallas_call(
        functools.partial(deal_kernel, (n_row, n_z, n_y, n_core)),
        out_shape=[jax.ShapeDtypeStruct((n_core, count, n_z * blk), BF16)] * n_plane,
        in_specs=[VMEM],
        out_specs=[VMEM] * n_plane,
        scratch_shapes=[pltpu.VMEM((n_plane, n_core, count, n_z * blk), BF16)],
        compiler_params=params(16 * MIB),
        name="deal",
    )(x_here)
    stacked = jnp.stack(kv_near)
    kv_all = [piece[None] for piece in kv_near] if n_pieces <= 8 else [stacked]
    kv_all = kv_all + [over_core(stacked)]

    tail_rows = 4 * -(-total // (8 * LANES)) * 8
    big = jax.ShapeDtypeStruct((n_pieces, count, total), BF16)
    lines = pl.pallas_call(
        functools.partial(lines_kernel, count, width, n_z),
        out_shape=[jax.ShapeDtypeStruct((total, width), BF16)] * 2
        + [jax.ShapeDtypeStruct((8, total), F32)],
        in_specs=[VMEM] * n_z,
        out_specs=[VMEM] * 3,
        compiler_params=params(8 * MIB),
        cost_estimate=pl.CostEstimate(flops=int(5e9), bytes_accessed=0, transcendentals=0),
        name="lines",
    )(*qg_all[::-1])
    w, u, stat, own_part, *send = pl.pallas_call(
        functools.partial(forward_kernel, count, width, n_z, len(kv_all)),
        out_shape=[
            big,
            big,
            jax.ShapeDtypeStruct((8, total), F32),
            jax.ShapeDtypeStruct((count, width), BF16),
        ]
        + [jax.ShapeDtypeStruct((count + tail_rows, width), BF16)] * (n_z - 1),
        in_specs=[VMEM] * (3 + len(kv_all)),
        out_specs=[VMEM] * (4 + n_z - 1),
        scratch_shapes=[
            pltpu.VMEM((n_pieces, count, width), BF16),
            pltpu.VMEM((n_pieces, count, width), BF16),
            pltpu.VMEM((n_pieces, count, 8), F32),
            pltpu.VMEM((math.gcd(n_pieces, 8), count, total), F32),
            pltpu.VMEM((math.gcd(n_pieces, 8), count, total), F32),
            pltpu.VMEM((total, width), BF16),
        ],
        compiler_params=params(24 * MIB if n_pieces <= 8 else 56 * MIB),
        cost_estimate=pl.CostEstimate(flops=int(3e10), bytes_accessed=0, transcendentals=0),
        name="forward",
    )(*lines, *kv_all)
    got = over_z(send)
    x_all = [x_send[0]] + [over_plane(x, where) for x, where in zip(x_send[1:], plane[1:])]
    far = [index for index, (a, b) in enumerate(plane) if a and b]
    near = [index for index, (a, b) in enumerate(plane) if (a or b) and not (a and b)]

    def together(values, indices):
        values, some = lax.optimization_barrier((values, [x_all[index] for index in indices]))
        for index, value in zip(indices, some):
            x_all[index] = value
        return values

    got = together(got, far)

    half = (n_plane, count, width)
    cut = cut_rows(count)
    other_k, other_v, queries_low, grads_low, shares = pl.pallas_call(
        functools.partial(away_kernel, count, width, n_z, plane, n_y),
        out_shape=[jax.ShapeDtypeStruct(half, BF16)] * 2
        + [jax.ShapeDtypeStruct((total, width), BF16)] * 2
        + [jax.ShapeDtypeStruct((total, 8), F32)],
        in_specs=[VMEM] * (5 + n_z - 1),
        out_specs=[VMEM] * 5,
        scratch_shapes=[pltpu.VMEM((8, total), F32)],
        compiler_params=params(16 * MIB if n_pieces <= 8 else 56 * MIB),
        cost_estimate=pl.CostEstimate(flops=int(3e10), bytes_accessed=0, transcendentals=0),
        name="away",
    )(w, u, stat, *lines[:2], *got[::-1])
    query_low, query_high = pl.pallas_call(
        query_kernel,
        out_shape=[
            jax.ShapeDtypeStruct((cut, width), BF16),
            jax.ShapeDtypeStruct((count - cut, width), BF16),
        ],
        in_specs=[VMEM] * (2 + n_z - 1),
        out_specs=[VMEM] * 2,
        compiler_params=params(8 * MIB),
        name="query",
    )(own_part, shares, *got)
    mine_k, mine_v = pl.pallas_call(
        functools.partial(home_kernel, plane, n_y),
        out_shape=[jax.ShapeDtypeStruct(half, F32 if n_pieces <= 8 else BF16)] * 2,
        in_specs=[VMEM] * 4,
        out_specs=[VMEM] * 2,
        compiler_params=params(16 * MIB if n_pieces <= 8 else 56 * MIB),
        name="home",
    )(w, u, queries_low, grads_low)
    mine_k, mine_v = together([mine_k, mine_v], near)
    key_sum = mine_k.astype(F32) + over_core(other_k).astype(F32)
    value_sum = mine_v.astype(F32) + over_core(other_v).astype(F32)
    x_pair = [over_core(x) for x in x_all]
    row_bits = [(1 << bit, 0) for bit in range(n_row.bit_length() - 1)]
    y_bits = [(0, 1 << bit) for bit in range(n_y.bit_length() - 1)]
    lows, highs = {(0, 0): query_low}, {(0, 0): query_high}
    body = n_plane * count

    def payload(sums, pieces):
        return jnp.concatenate([sums.astype(BF16).reshape(body, width), *pieces.values()])

    def take(sums, pieces, got, hop, rows):
        for index, (a, b) in enumerate(list(pieces)):
            first = body + index * rows
            pieces[a ^ hop[0], b ^ hop[1]] = got[first : first + rows]
        return sums + got[:body].reshape(half).astype(F32)

    for key_hop, value_hop in zip(row_bits + y_bits, y_bits + row_bits):
        sent = lax.optimization_barrier((payload(key_sum, lows), payload(value_sum, highs)))
        key_got, value_got = lax.optimization_barrier(
            (over_plane(sent[0], key_hop), over_plane(sent[1], value_hop))
        )
        key_sum = take(key_sum, lows, key_got, key_hop, cut)
        value_sum = take(value_sum, highs, value_got, value_hop, count - cut)
    place = plane_places(plane, n_y)[0]
    key_low, value_low = key_sum.astype(BF16), value_sum.astype(BF16)
    key_grad = lax.dynamic_index_in_dim(key_low, place, 0, False)
    value_grad = lax.dynamic_index_in_dim(value_low, place, 0, False)
    query_all = [pieces[where] for pieces in (lows, highs) for where in plane]
    g_near = [jnp.concatenate(query_all), key_low, value_low]
    g_far = [over_core(g) for g in g_near]

    tokens = n_plane * count
    operands = [pltpu.VMEM((tokens, n_z * blk), BF16), pltpu.VMEM((tokens, 3 * width), BF16)]
    near_sum = pl.pallas_call(
        functools.partial(near_kernel, plane, n_y),
        out_shape=jax.ShapeDtypeStruct((n_z * blk, 3 * width), F32),
        in_specs=[VMEM] * (n_plane + 3),
        out_specs=VMEM,
        scratch_shapes=operands,
        compiler_params=params(24 * MIB),
        name="near",
    )(*x_all, *g_near)
    mine, *send = pl.pallas_call(
        functools.partial(far_kernel, plane, n_y, n_z),
        out_shape=[jax.ShapeDtypeStruct((blk, 3 * width), F32)]
        + [jax.ShapeDtypeStruct((blk, 3 * width), BF16)] * (n_z - 1),
        in_specs=[VMEM] * (n_plane + 4),
        out_specs=[VMEM] * n_z,
        scratch_shapes=operands + [pltpu.VMEM((n_z, blk, 3 * width), F32)],
        compiler_params=params(24 * MIB),
        name="far",
    )(near_sum, *x_pair, *g_far)
    mine, query_low, query_high = lax.optimization_barrier((mine, query_low, query_high))
    both = [mine] + send
    piece = both[0]
    for part in over_z(both[1:]):
        piece = piece + part.astype(F32)
    low = piece.astype(BF16)
    parts = [piece] + [xor_permute(low, ("row",), (a,)) for a in range(1, n_row)]
    weight_grad = pl.pallas_call(
        assemble_kernel,
        out_shape=jax.ShapeDtypeStruct((n_row, blk, 3 * width), F32),
        in_specs=[VMEM] * n_row,
        out_specs=VMEM,
        compiler_params=params(8 * MIB),
        name="assemble",
    )(*parts).reshape(n_row * blk, 3 * width)
    query_grad = jnp.concatenate([query_low, query_high])
    return query_grad, key_grad, value_grad, weight_grad


def solution(mesh):
    n_row, n_col = mesh.shape["row"], mesh.shape["col"]
    n_core = 2
    n_z = 1 << ((n_col.bit_length() - 1) // 2)
    n_y = n_col // (n_core * n_z)
    axes = (("row", n_row), ("z", n_z), ("y", n_y), ("core", n_core))
    split = Mesh(
        mesh.devices.reshape(tuple(size for _, size in axes)), tuple(name for name, _ in axes)
    )
    tokens = P(("row", "z", "y", "core"), None)
    return jax.shard_map(
        functools.partial(local, axes),
        mesh=split,
        in_specs=(tokens,) * 6 + (P(), P()),
        out_specs=(tokens, tokens, tokens, P(("z", "y", "core"), None)),
        check_vma=False,
    )
```

```python
import functools
import math

import jax
import jax.numpy as jnp
from jax import lax
from jax.experimental import pallas as pl
from jax.experimental.pallas import tpu as pltpu
from jax.sharding import Mesh
from jax.sharding import PartitionSpec as P

BLK = 128
LANES = 128
PAD_ROWS = 16
NEG_FILL = -1e30
LOG2E = math.log2(math.e)
MIB = 1 << 20
F32 = jnp.float32
BF16 = jnp.bfloat16
VMEM = pl.BlockSpec(memory_space=pltpu.VMEM)
HBM = pl.BlockSpec(memory_space=pltpu.HBM)


def cut_rows(count):
    return count * 9 // (10 * PAD_ROWS) * PAD_ROWS


def plane_places(plane, n_y):
    row_id, y_id = lax.axis_index("row"), lax.axis_index("y")
    return [(row_id ^ a) * n_y + (y_id ^ b) for a, b in plane]


def dot_nt(left, right, precision=None):
    return lax.dot_general(
        left, right, (((1,), (1,)), ((), ())), preferred_element_type=F32, precision=precision
    )


def dot_tn(left, right):
    return lax.dot_general(left, right, (((0,), (0,)), ((), ())), preferred_element_type=F32)


def params(nbytes):
    return pltpu.CompilerParams(vmem_limit_bytes=nbytes)


def split_three(values):
    high = values.astype(BF16).astype(F32)
    rest = values - high
    middle = rest.astype(BF16).astype(F32)
    return high, middle, rest - middle


def pack_kernel(
    axes, q_hbm, k_hbm, v_hbm, o_hbm, g_hbm, x_hbm, pos_hbm, ids_hbm, qg_ref, kv_ref, x_ref, *scratch
):
    outs, prod, extra, pos, ids, sems = scratch
    count, width = outs.shape
    copies = [
        pltpu.make_async_copy(source, target, sems.at[place])
        for place, (source, target) in enumerate(
            (
                (pos_hbm, pos),
                (ids_hbm, ids),
                (g_hbm, qg_ref.at[:count, width:]),
                (o_hbm, outs),
                (q_hbm, qg_ref.at[:count, :width]),
                (k_hbm, kv_ref.at[:count, :width]),
                (v_hbm, kv_ref.at[:count, width:]),
                (x_hbm, x_ref),
            )
        )
    ]
    for copy in copies:
        copy.start()
    me = jnp.int32(0)
    for name, size in axes:
        me = me * size + lax.axis_index(name)
    prod[...] = jnp.zeros_like(prod)
    copies[0].wait()
    copies[1].wait()
    lines = min(pos.shape[0], (count + LANES - 2) // LANES + 1)
    first = jnp.minimum(me * count // LANES, pos.shape[0] - lines)
    shift = me * count - first * LANES
    block = jnp.concatenate([pos[pl.ds(first + i, 1), :] for i in range(lines)], axis=1) // BLK

    def add_id(index, found):
        return jnp.where(block == index, ids[index], found)

    found = lax.fori_loop(0, ids.shape[0], add_id, jnp.zeros_like(block), unroll=8)
    found = jnp.broadcast_to(found.astype(F32), (8, lines * LANES))
    found = pltpu.roll(found, lines * LANES - shift, 1)
    copies[2].wait()
    copies[3].wait()
    prod[:count, :] = qg_ref[:count, width:].astype(F32) * outs[...].astype(F32)
    delta = dot_nt(
        jnp.ones((PAD_ROWS, width), F32), prod[...], precision=lax.Precision.HIGHEST
    )
    high, middle, low = split_three(delta)
    row = lax.broadcasted_iota(jnp.int32, delta.shape, 0)
    extra[...] = jnp.where(row == 0, high, jnp.where(row == 1, middle, jnp.where(row == 2, low, 0.0)))
    extra[3:4, :count] = found[0:1, :count]
    tail = extra[...].astype(BF16)
    qg_ref[count:, :] = tail
    kv_ref[count:, :] = tail
    for copy in copies[4:]:
        copy.wait()


def deal_kernel(sizes, x_ref, *refs):
    *out_refs, dealt = refs
    n_row, n_z, n_y, n_core = sizes
    blk = x_ref.shape[1] // (n_row * n_z * n_y * n_core)
    for a in range(n_row):
        for b in range(n_y):
            for core in range(n_core):
                for z in range(n_z):
                    first = (((z * n_y + b) * n_core + core) * n_row + a) * blk
                    dealt[a * n_y + b, core, :, z * blk : (z + 1) * blk] = x_ref[:, first : first + blk]
    me_row, me_y = lax.axis_index("row"), lax.axis_index("y")
    for a in range(n_row):
        for b in range(n_y):
            out_refs[a * n_y + b][...] = dealt[(me_row ^ a) * n_y + (me_y ^ b)]


def assemble_kernel(own_ref, *refs):
    *got_refs, out_ref = refs
    me_row = lax.axis_index("row")
    out_ref[me_row] = own_ref[...]
    for offset, ref in enumerate(got_refs, 1):
        out_ref[me_row ^ offset] = ref[...].astype(F32)


def line_rows(slot, count):
    place = lax.axis_index("z") ^ slot
    return pl.ds(pl.multiple_of(place * count, PAD_ROWS), count)


def lines_kernel(count, width, n_q, *refs):
    qg_refs, (queries, grads, rows) = refs[:n_q][::-1], refs[n_q:]
    z_id = lax.axis_index("z")
    for slot, ref in enumerate(qg_refs):
        queries[line_rows(slot, count), :] = ref[:count, :width]
        grads[line_rows(slot, count), :] = ref[:count, width:]
    tails = [ref[count:, :].astype(F32) for ref in qg_refs]
    deltas = [(tail[0:1] + tail[1:2] + tail[2:3])[:, :count] for tail in tails]
    samples = [tail[3:4, :count] for tail in tails]
    for place in range(n_q):
        where = slice(place * count, (place + 1) * count)
        delta, sample = deltas[0], samples[0]
        for slot in range(1, n_q):
            here = (z_id ^ slot) == place
            delta = jnp.where(here, deltas[slot], delta)
            sample = jnp.where(here, samples[slot], sample)
        rows[0:1, where] = delta
        rows[1:2, where] = sample


def forward_kernel(count, width, n_q, n_kv, *refs):
    queries, grads, lines, refs = *refs[:3], refs[3:]
    kv_refs, refs = refs[:n_kv], refs[n_kv:]
    w_ref, u_ref, stat_ref, own_ref, refs = *refs[:4], refs[4:]
    send_refs, (keys, values, samples, scores, slopes, parts) = refs[: n_q - 1], refs[n_q - 1 :]
    total = n_q * count
    factor = LOG2E / math.sqrt(width)
    delta, query_samples = lines[0:1, :], lines[1:2, :]
    n_pieces = w_ref.shape[0]
    block = scores.shape[0]
    n_blocks = n_pieces // block

    def load(ref, index):
        keys[index] = ref[:count, :width]
        values[index] = ref[:count, width:]
        samples[index] = jnp.transpose(ref[count:, :].astype(F32))[:count, :8]

    base = 0
    for ref in kv_refs:
        depth = ref.shape[0]
        if depth <= 4:
            for i in range(depth):
                load(ref.at[i], base + i)
        else:

            @pl.loop(0, depth)
            def _(i, ref=ref, base=base):
                load(ref.at[i], base + i)

        base += depth

    def over_blocks(body, state):
        if n_blocks == 1:
            return body(0, state)
        return lax.fori_loop(0, n_blocks, lambda i, s: body(i * block, s), state)

    def fold(part, combine):
        out = part[0:8]
        for start in range(8, count, 8):
            out = combine(out, part[start : start + 8])
        return out

    def product(left, right, first):
        left = left[pl.ds(first, block)].reshape(block * count, width)
        return dot_nt(left, right[...]).reshape(block, count, total)

    def peak_step(first, peak):
        scores[...] = product(keys, queries, first)
        if n_blocks == 1:
            slopes[...] = product(values, grads, first)
        for piece in range(block):
            live = samples[first + piece][:, 3:4] == query_samples
            masked = jnp.where(live, scores[piece], NEG_FILL)
            scores[piece] = masked
            peak = jnp.maximum(peak, fold(masked, jnp.maximum))
        return peak

    turned = jnp.transpose(keys[:block].reshape(block * count, width))

    peak8 = over_blocks(peak_step, jnp.full((8, total), NEG_FILL, F32))
    peak = jnp.max(peak8, axis=0, keepdims=True)

    def grad_step(first, mass):
        if n_blocks > 1:
            peak_step(first, peak8)
            slopes[...] = product(values, grads, first)
        for piece in range(block):
            weight = jnp.exp2((scores[piece] - peak) * factor)
            w_ref[first + piece] = weight.astype(BF16)
            u_ref[first + piece] = (weight * (slopes[piece] - delta)).astype(BF16)
            mass = mass + fold(weight, jnp.add)
            if n_blocks == 1 and (piece + 1) % 4 == 0:
                rows = 4 * count
                first_row = (piece + 1) * count - rows
                known = u_ref[piece + 1 - 4 : piece + 1].reshape(rows, total)
                left = turned[:, first_row : first_row + rows]
                joins.append(jnp.dot(left, known, preferred_element_type=F32))
        return mass

    joins = []
    mass8 = over_blocks(grad_step, jnp.zeros((8, total), F32))
    mass = jnp.sum(mass8, axis=0, keepdims=True)
    level = peak * factor + jnp.log2(mass)
    stat_ref[...] = jnp.zeros_like(stat_ref)
    stat_ref[0:1, :] = peak * factor
    stat_ref[1:2, :] = level

    def join_step(first, joined):
        rows = block * count
        return joined + dot_tn(
            keys[pl.ds(first, block)].reshape(rows, width),
            u_ref[pl.ds(first, block)].reshape(rows, total),
        )

    if n_blocks == 1:
        joined = functools.reduce(jnp.add, joins)
    else:
        joined = over_blocks(join_step, jnp.zeros((width, total), F32))
    parts[...] = jnp.transpose((joined * (1.0 / mass)).astype(BF16))
    own_ref[...] = parts[line_rows(0, count), :]
    tail_rows = send_refs[0].shape[0] - count
    step = tail_rows // 4
    row = lax.broadcasted_iota(jnp.int32, (tail_rows, LANES), 0)
    tail = jnp.zeros((tail_rows, LANES), F32)
    for index, part in enumerate(split_three(level)):
        for chunk in range(total // LANES):
            line = part[:, chunk * LANES : (chunk + 1) * LANES]
            tail = jnp.where(row == index * step + chunk, line, tail)
    for offset, ref in enumerate(send_refs, 1):
        ref[:count, :] = parts[line_rows(offset, count), :]
        ref[count:, :] = tail.astype(BF16)


def products(w_ref, u_ref, first, size, places, queries, grads, key_ref, value_ref, scale):
    _, count, total = w_ref.shape
    many, shape = (size * count, total), (size, count, key_ref.shape[2])
    value_part = jnp.dot(
        w_ref[pl.ds(first, size)].reshape(many), grads[...], preferred_element_type=F32
    ).reshape(shape)
    key_part = jnp.dot(
        u_ref[pl.ds(first, size)].reshape(many), queries[...], preferred_element_type=F32
    ).reshape(shape)
    for step, place in enumerate(places):
        key_ref[place] = (key_part[step] * scale).astype(key_ref.dtype)
        value_ref[place] = value_part[step].astype(value_ref.dtype)


def away_kernel(count, width, n_q, plane, n_y, *refs):
    w_ref, u_ref, stat_ref, all_queries, all_grads, refs = *refs[:5], refs[5:]
    got_refs, refs = refs[: n_q - 1][::-1], refs[n_q - 1 :]
    other_k_ref, other_v_ref, queries, grads, shares_ref, table = refs
    chunks = n_q * count // LANES
    scale = 1.0 / math.sqrt(width)
    levels = [stat_ref[1:2, :]]
    for ref in got_refs:
        tail = ref[count:, :].astype(F32)
        step = tail.shape[0] // 4
        summed = tail[:step] + tail[step : 2 * step] + tail[2 * step : 3 * step]
        levels.append(jnp.concatenate([summed[c : c + 1] for c in range(chunks)], axis=1))
    top = functools.reduce(jnp.maximum, levels)
    shares = [jnp.exp2(one - top) for one in levels]
    inverse = 1.0 / functools.reduce(jnp.add, shares)
    table[...] = jnp.zeros_like(table)
    table[0:1, :] = jnp.exp2(stat_ref[0:1, :] - top) * inverse
    for index, share in enumerate(shares, 1):
        table[index : index + 1, :] = share * inverse * scale
    columns = jnp.transpose(table[...])
    shares_ref[...] = columns
    queries[...] = (all_queries[...].astype(F32) * columns[:, 0:1]).astype(BF16)
    grads[...] = (all_grads[...].astype(F32) * columns[:, 0:1]).astype(BF16)
    half = w_ref.shape[0] // 2
    places = plane_places(plane, n_y)
    if half <= 4:
        products(
            w_ref, u_ref, half, half, places, queries, grads, other_k_ref, other_v_ref, scale
        )
    else:
        for i, place in enumerate(places):
            products(
                w_ref, u_ref, half + i, 1, [place], queries, grads, other_k_ref, other_v_ref, scale
            )


def query_kernel(own_ref, shares_ref, *refs):
    *got_refs, low_ref, high_ref = refs
    count, _ = own_ref.shape
    own = shares_ref[line_rows(0, count), :]
    query_grad = own_ref[...].astype(F32) * own[:, 1:2]
    for index, ref in enumerate(got_refs, 2):
        query_grad = query_grad + ref[:count, :].astype(F32) * own[:, index : index + 1]
    cut = low_ref.shape[0]
    low_ref[...] = query_grad[:cut].astype(BF16)
    high_ref[...] = query_grad[cut:].astype(BF16)


def home_kernel(plane, n_y, w_ref, u_ref, queries, grads, key_ref, value_ref):
    half = w_ref.shape[0] // 2
    places = plane_places(plane, n_y)
    scale = 1.0 / math.sqrt(queries.shape[1])
    if half <= 4:
        products(w_ref, u_ref, 0, half, places, queries, grads, key_ref, value_ref, scale)
    else:
        for i, place in enumerate(places):
            products(w_ref, u_ref, i, 1, [place], queries, grads, key_ref, value_ref, scale)


def token_product(plane, n_y, x_refs, g_refs, inputs, grads):
    query_ref, key_ref, value_ref = g_refs
    n_plane = len(plane)
    count, width = key_ref.shape[1:]
    cut = cut_rows(count)
    high, rest = n_plane * cut, count - cut
    core_id = lax.axis_index("core")
    for slot, place in enumerate(plane_places(plane, n_y)):
        rows = slice(slot * count, (slot + 1) * count)
        inputs[rows, :] = x_refs[slot][core_id]
        middle = slot * count + cut
        grads[slot * count : middle, :width] = query_ref[slot * cut : (slot + 1) * cut, :]
        grads[middle : (slot + 1) * count, :width] = query_ref[
            high + slot * rest : high + (slot + 1) * rest, :
        ]
        grads[rows, width : 2 * width] = key_ref[place]
        grads[rows, 2 * width :] = value_ref[place]
    return dot_tn(inputs[...], grads[...])


def near_kernel(plane, n_y, *refs):
    x_refs, g_refs = refs[: len(plane)], refs[len(plane) : len(plane) + 3]
    sum_ref, inputs, grads = refs[len(plane) + 3 :]
    sum_ref[...] = token_product(plane, n_y, x_refs, g_refs, inputs, grads)


def far_kernel(plane, n_y, n_z, near_ref, *refs):
    x_refs, g_refs = refs[: len(plane)], refs[len(plane) : len(plane) + 3]
    refs = refs[len(plane) + 3 :]
    out_refs, (inputs, grads, sums) = refs[:n_z], refs[n_z:]
    total = near_ref[...] + token_product(plane, n_y, x_refs, g_refs, inputs, grads)
    sums[...] = total.reshape(sums.shape)
    z_id = lax.axis_index("z")
    for slot, ref in enumerate(out_refs):
        ref[...] = sums[z_id ^ slot].astype(ref.dtype)


def xor_permute(value, names, offsets):
    sizes = [lax.axis_size(name) for name in names]
    pairs = []
    for source in range(math.prod(sizes)):
        rest, digits = source, []
        for size in reversed(sizes):
            digits.append(rest % size)
            rest //= size
        target = 0
        for digit, size, offset in zip(reversed(digits), sizes, offsets):
            target = target * size + (digit ^ offset)
        pairs.append((source, target))
    return lax.ppermute(value, tuple(names), pairs)


def local(axes, layer_input, queries, keys, values, forward_out, out_grad, token_pos, block_sample):
    sizes = dict(axes)
    n_row, n_z, n_y, n_core = (sizes[name] for name in ("row", "z", "y", "core"))
    count, width = queries.shape
    model_width = layer_input.shape[1]
    total = n_z * count
    plane = [(a, b) for a in range(n_row) for b in range(n_y)]
    n_plane = len(plane)
    n_pieces = n_core * n_plane

    def over_plane(value, where):
        return xor_permute(value, ("row", "y"), where)

    def over_z(values):
        far_first = reversed(list(enumerate(values, 1)))
        return [xor_permute(value, ("z",), (offset,)) for offset, value in far_first][::-1]

    def over_core(value):
        return xor_permute(value, ("core",), (1,))

    packed = jax.ShapeDtypeStruct((count + PAD_ROWS, 2 * width), BF16)
    qg, kv, x_here = pl.pallas_call(
        functools.partial(pack_kernel, axes),
        out_shape=(packed, packed, jax.ShapeDtypeStruct(layer_input.shape, BF16)),
        in_specs=[HBM] * 8,
        out_specs=(VMEM, VMEM, VMEM),
        scratch_shapes=[
            pltpu.VMEM((count, width), BF16),
            pltpu.VMEM((2 * width, width), F32),
            pltpu.VMEM((PAD_ROWS, 2 * width), F32),
            pltpu.VMEM((token_pos.shape[0] // LANES, LANES), jnp.int32),
            pltpu.SMEM(block_sample.shape, jnp.int32),
            pltpu.SemaphoreType.DMA((8,)),
        ],
        compiler_params=params(8 * MIB),
        name="pack",
    )(
        *(
            pltpu.with_memory_space_constraint(value, pltpu.HBM)
            for value in (
                queries,
                keys,
                values,
                forward_out,
                out_grad,
                layer_input,
                token_pos.reshape(-1, LANES),
                block_sample,
            )
        )
    )

    blk = model_width // (n_z * n_y * n_core * n_row)
    kv_near = [kv] + [over_plane(kv, where) for where in plane[1:]]
    qg_all = [qg] + over_z([qg] * (n_z - 1))
    x_here, kv_near[1] = lax.optimization_barrier((x_here, kv_near[1]))
    x_send = pl.pallas_call(
        functools.partial(deal_kernel, (n_row, n_z, n_y, n_core)),
        out_shape=[jax.ShapeDtypeStruct((n_core, count, n_z * blk), BF16)] * n_plane,
        in_specs=[VMEM],
        out_specs=[VMEM] * n_plane,
        scratch_shapes=[pltpu.VMEM((n_plane, n_core, count, n_z * blk), BF16)],
        compiler_params=params(16 * MIB),
        name="deal",
    )(x_here)
    stacked = jnp.stack(kv_near)
    kv_all = [piece[None] for piece in kv_near] if n_pieces <= 8 else [stacked]
    kv_all = kv_all + [over_core(stacked)]

    tail_rows = 4 * -(-total // (8 * LANES)) * 8
    big = jax.ShapeDtypeStruct((n_pieces, count, total), BF16)
    lines = pl.pallas_call(
        functools.partial(lines_kernel, count, width, n_z),
        out_shape=[jax.ShapeDtypeStruct((total, width), BF16)] * 2
        + [jax.ShapeDtypeStruct((8, total), F32)],
        in_specs=[VMEM] * n_z,
        out_specs=[VMEM] * 3,
        compiler_params=params(8 * MIB),
        cost_estimate=pl.CostEstimate(flops=int(5e9), bytes_accessed=0, transcendentals=0),
        name="lines",
    )(*qg_all[::-1])
    w, u, stat, own_part, *send = pl.pallas_call(
        functools.partial(forward_kernel, count, width, n_z, len(kv_all)),
        out_shape=[
            big,
            big,
            jax.ShapeDtypeStruct((8, total), F32),
            jax.ShapeDtypeStruct((count, width), BF16),
        ]
        + [jax.ShapeDtypeStruct((count + tail_rows, width), BF16)] * (n_z - 1),
        in_specs=[VMEM] * (3 + len(kv_all)),
        out_specs=[VMEM] * (4 + n_z - 1),
        scratch_shapes=[
            pltpu.VMEM((n_pieces, count, width), BF16),
            pltpu.VMEM((n_pieces, count, width), BF16),
            pltpu.VMEM((n_pieces, count, 8), F32),
            pltpu.VMEM((math.gcd(n_pieces, 8), count, total), F32),
            pltpu.VMEM((math.gcd(n_pieces, 8), count, total), F32),
            pltpu.VMEM((total, width), BF16),
        ],
        compiler_params=params(24 * MIB if n_pieces <= 8 else 56 * MIB),
        cost_estimate=pl.CostEstimate(flops=int(3e10), bytes_accessed=0, transcendentals=0),
        name="forward",
    )(*lines, *kv_all)
    got = over_z(send)
    x_all = [x_send[0]] + [over_plane(x, where) for x, where in zip(x_send[1:], plane[1:])]
    far = [index for index, (a, b) in enumerate(plane) if a and b]
    near = [index for index, (a, b) in enumerate(plane) if (a or b) and not (a and b)]

    def together(values, indices):
        values, some = lax.optimization_barrier((values, [x_all[index] for index in indices]))
        for index, value in zip(indices, some):
            x_all[index] = value
        return values

    got = together(got, far)

    half = (n_plane, count, width)
    cut = cut_rows(count)
    other_k, other_v, queries_low, grads_low, shares = pl.pallas_call(
        functools.partial(away_kernel, count, width, n_z, plane, n_y),
        out_shape=[jax.ShapeDtypeStruct(half, BF16)] * 2
        + [jax.ShapeDtypeStruct((total, width), BF16)] * 2
        + [jax.ShapeDtypeStruct((total, 8), F32)],
        in_specs=[VMEM] * (5 + n_z - 1),
        out_specs=[VMEM] * 5,
        scratch_shapes=[pltpu.VMEM((8, total), F32)],
        compiler_params=params(16 * MIB if n_pieces <= 8 else 56 * MIB),
        cost_estimate=pl.CostEstimate(flops=int(3e10), bytes_accessed=0, transcendentals=0),
        name="away",
    )(w, u, stat, *lines[:2], *got[::-1])
    query_low, query_high = pl.pallas_call(
        query_kernel,
        out_shape=[
            jax.ShapeDtypeStruct((cut, width), BF16),
            jax.ShapeDtypeStruct((count - cut, width), BF16),
        ],
        in_specs=[VMEM] * (2 + n_z - 1),
        out_specs=[VMEM] * 2,
        compiler_params=params(8 * MIB),
        name="query",
    )(own_part, shares, *got)
    mine_k, mine_v = pl.pallas_call(
        functools.partial(home_kernel, plane, n_y),
        out_shape=[jax.ShapeDtypeStruct(half, F32 if n_pieces <= 8 else BF16)] * 2,
        in_specs=[VMEM] * 4,
        out_specs=[VMEM] * 2,
        compiler_params=params(16 * MIB if n_pieces <= 8 else 56 * MIB),
        name="home",
    )(w, u, queries_low, grads_low)
    mine_k, mine_v = together([mine_k, mine_v], near)
    key_sum = mine_k.astype(F32) + over_core(other_k).astype(F32)
    value_sum = mine_v.astype(F32) + over_core(other_v).astype(F32)
    x_pair = [over_core(x) for x in x_all]
    row_bits = [(1 << bit, 0) for bit in range(n_row.bit_length() - 1)]
    y_bits = [(0, 1 << bit) for bit in range(n_y.bit_length() - 1)]
    lows, highs = {(0, 0): query_low}, {(0, 0): query_high}
    body = n_plane * count

    def payload(sums, pieces):
        return jnp.concatenate([sums.astype(BF16).reshape(body, width), *pieces.values()])

    def take(sums, pieces, got, hop, rows):
        for index, (a, b) in enumerate(list(pieces)):
            first = body + index * rows
            pieces[a ^ hop[0], b ^ hop[1]] = got[first : first + rows]
        return sums + got[:body].reshape(half).astype(F32)

    for key_hop, value_hop in zip(row_bits + y_bits, y_bits + row_bits):
        sent = lax.optimization_barrier((payload(key_sum, lows), payload(value_sum, highs)))
        key_got, value_got = lax.optimization_barrier(
            (over_plane(sent[0], key_hop), over_plane(sent[1], value_hop))
        )
        key_sum = take(key_sum, lows, key_got, key_hop, cut)
        value_sum = take(value_sum, highs, value_got, value_hop, count - cut)
    place = plane_places(plane, n_y)[0]
    key_low, value_low = key_sum.astype(BF16), value_sum.astype(BF16)
    key_grad = lax.dynamic_index_in_dim(key_low, place, 0, False)
    value_grad = lax.dynamic_index_in_dim(value_low, place, 0, False)
    query_all = [pieces[where] for pieces in (lows, highs) for where in plane]
    g_near = [jnp.concatenate(query_all), key_low, value_low]
    g_far = [over_core(g) for g in g_near]

    tokens = n_plane * count
    operands = [pltpu.VMEM((tokens, n_z * blk), BF16), pltpu.VMEM((tokens, 3 * width), BF16)]
    near_sum = pl.pallas_call(
        functools.partial(near_kernel, plane, n_y),
        out_shape=jax.ShapeDtypeStruct((n_z * blk, 3 * width), F32),
        in_specs=[VMEM] * (n_plane + 3),
        out_specs=VMEM,
        scratch_shapes=operands,
        compiler_params=params(24 * MIB),
        name="near",
    )(*x_all, *g_near)
    mine, *send = pl.pallas_call(
        functools.partial(far_kernel, plane, n_y, n_z),
        out_shape=[jax.ShapeDtypeStruct((blk, 3 * width), F32)]
        + [jax.ShapeDtypeStruct((blk, 3 * width), BF16)] * (n_z - 1),
        in_specs=[VMEM] * (n_plane + 4),
        out_specs=[VMEM] * n_z,
        scratch_shapes=operands + [pltpu.VMEM((n_z, blk, 3 * width), F32)],
        compiler_params=params(24 * MIB),
        name="far",
    )(near_sum, *x_pair, *g_far)
    mine, query_low, query_high = lax.optimization_barrier((mine, query_low, query_high))
    both = [mine] + send
    piece = both[0]
    for part in over_z(both[1:]):
        piece = piece + part.astype(F32)
    low = piece.astype(BF16)
    parts = [piece] + [xor_permute(low, ("row",), (a,)) for a in range(1, n_row)]
    weight_grad = pl.pallas_call(
        assemble_kernel,
        out_shape=jax.ShapeDtypeStruct((n_row, blk, 3 * width), F32),
        in_specs=[VMEM] * n_row,
        out_specs=VMEM,
        compiler_params=params(8 * MIB),
        name="assemble",
    )(*parts).reshape(n_row * blk, 3 * width)
    query_grad = jnp.concatenate([query_low, query_high])
    return query_grad, key_grad, value_grad, weight_grad


def solution(mesh):
    n_row, n_col = mesh.shape["row"], mesh.shape["col"]
    n_core = 2
    n_z = 1 << ((n_col.bit_length() - 1) // 2)
    n_y = n_col // (n_core * n_z)
    axes = (("row", n_row), ("z", n_z), ("y", n_y), ("core", n_core))
    split = Mesh(
        mesh.devices.reshape(tuple(size for _, size in axes)), tuple(name for name, _ in axes)
    )
    tokens = P(("row", "z", "y", "core"), None)
    return jax.shard_map(
        functools.partial(local, axes),
        mesh=split,
        in_specs=(tokens,) * 6 + (P(), P()),
        out_specs=(tokens, tokens, tokens, P(("z", "y", "core"), None)),
        check_vma=False,
    )
```

```python
import functools
import math

import jax
import jax.numpy as jnp
from jax import lax
from jax.experimental import pallas as pl
from jax.experimental.pallas import tpu as pltpu
from jax.sharding import Mesh
from jax.sharding import PartitionSpec as P

BLK = 128
LANES = 128
PAD_ROWS = 16
NEG_FILL = -1e30
LOG2E = math.log2(math.e)
MIB = 1 << 20
F32 = jnp.float32
BF16 = jnp.bfloat16
VMEM = pl.BlockSpec(memory_space=pltpu.VMEM)
HBM = pl.BlockSpec(memory_space=pltpu.HBM)


def cut_rows(count):
    return count * 9 // (10 * PAD_ROWS) * PAD_ROWS


def plane_places(plane, n_y):
    row_id, y_id = lax.axis_index("row"), lax.axis_index("y")
    return [(row_id ^ a) * n_y + (y_id ^ b) for a, b in plane]


def dot_nt(left, right, precision=None):
    return lax.dot_general(
        left, right, (((1,), (1,)), ((), ())), preferred_element_type=F32, precision=precision
    )


def dot_tn(left, right):
    return lax.dot_general(left, right, (((0,), (0,)), ((), ())), preferred_element_type=F32)


def params(nbytes):
    return pltpu.CompilerParams(vmem_limit_bytes=nbytes)


def split_three(values):
    high = values.astype(BF16).astype(F32)
    rest = values - high
    middle = rest.astype(BF16).astype(F32)
    return high, middle, rest - middle


def pack_kernel(
    axes, q_hbm, k_hbm, v_hbm, o_hbm, g_hbm, pos_hbm, ids_hbm, qg_ref, kv_ref, *scratch
):
    outs, prod, extra, pos, ids, sems = scratch
    count, width = outs.shape
    copies = [
        pltpu.make_async_copy(source, target, sems.at[place])
        for place, (source, target) in enumerate(
            (
                (pos_hbm, pos),
                (ids_hbm, ids),
                (g_hbm, qg_ref.at[:count, width:]),
                (o_hbm, outs),
                (q_hbm, qg_ref.at[:count, :width]),
                (k_hbm, kv_ref.at[:count, :width]),
                (v_hbm, kv_ref.at[:count, width:]),
            )
        )
    ]
    for copy in copies:
        copy.start()
    me = jnp.int32(0)
    for name, size in axes:
        me = me * size + lax.axis_index(name)
    prod[...] = jnp.zeros_like(prod)
    copies[0].wait()
    copies[1].wait()
    lines = min(pos.shape[0], (count + LANES - 2) // LANES + 1)
    first = jnp.minimum(me * count // LANES, pos.shape[0] - lines)
    shift = me * count - first * LANES
    block = jnp.concatenate([pos[pl.ds(first + i, 1), :] for i in range(lines)], axis=1) // BLK

    def add_id(index, found):
        return jnp.where(block == index, ids[index], found)

    found = lax.fori_loop(0, ids.shape[0], add_id, jnp.zeros_like(block), unroll=8)
    found = jnp.broadcast_to(found.astype(F32), (8, lines * LANES))
    found = pltpu.roll(found, lines * LANES - shift, 1)
    copies[2].wait()
    copies[3].wait()
    prod[:count, :] = qg_ref[:count, width:].astype(F32) * outs[...].astype(F32)
    delta = dot_nt(
        jnp.ones((PAD_ROWS, width), F32), prod[...], precision=lax.Precision.HIGHEST
    )
    high, middle, low = split_three(delta)
    row = lax.broadcasted_iota(jnp.int32, delta.shape, 0)
    extra[...] = jnp.where(row == 0, high, jnp.where(row == 1, middle, jnp.where(row == 2, low, 0.0)))
    extra[3:4, :count] = found[0:1, :count]
    tail = extra[...].astype(BF16)
    qg_ref[count:, :] = tail
    kv_ref[count:, :] = tail
    for copy in copies[4:]:
        copy.wait()


def deal_kernel(sizes, x_hbm, *refs):
    *out_refs, dealt, x_ref, sem = refs
    copy = pltpu.make_async_copy(x_hbm, x_ref, sem)
    copy.start()
    copy.wait()
    n_row, n_z, n_y, n_core = sizes
    blk = x_ref.shape[1] // (n_row * n_z * n_y * n_core)
    for a in range(n_row):
        for b in range(n_y):
            for core in range(n_core):
                for z in range(n_z):
                    first = (((z * n_y + b) * n_core + core) * n_row + a) * blk
                    dealt[a * n_y + b, core, :, z * blk : (z + 1) * blk] = x_ref[:, first : first + blk]
    me_row, me_y = lax.axis_index("row"), lax.axis_index("y")
    for a in range(n_row):
        for b in range(n_y):
            out_refs[a * n_y + b][...] = dealt[(me_row ^ a) * n_y + (me_y ^ b)]


def assemble_kernel(own_ref, *refs):
    *got_refs, out_ref = refs
    me_row = lax.axis_index("row")
    out_ref[me_row] = own_ref[...]
    for offset, ref in enumerate(got_refs, 1):
        out_ref[me_row ^ offset] = ref[...].astype(F32)


def line_rows(slot, count):
    place = lax.axis_index("z") ^ slot
    return pl.ds(pl.multiple_of(place * count, PAD_ROWS), count)


def lines_kernel(count, width, n_q, *refs):
    qg_refs, (queries, grads, rows) = refs[:n_q][::-1], refs[n_q:]
    z_id = lax.axis_index("z")
    for slot, ref in enumerate(qg_refs):
        queries[line_rows(slot, count), :] = ref[:count, :width]
        grads[line_rows(slot, count), :] = ref[:count, width:]
    tails = [ref[count:, :].astype(F32) for ref in qg_refs]
    deltas = [(tail[0:1] + tail[1:2] + tail[2:3])[:, :count] for tail in tails]
    samples = [tail[3:4, :count] for tail in tails]
    for place in range(n_q):
        where = slice(place * count, (place + 1) * count)
        delta, sample = deltas[0], samples[0]
        for slot in range(1, n_q):
            here = (z_id ^ slot) == place
            delta = jnp.where(here, deltas[slot], delta)
            sample = jnp.where(here, samples[slot], sample)
        rows[0:1, where] = delta
        rows[1:2, where] = sample


def forward_kernel(count, width, n_q, n_kv, *refs):
    queries, grads, lines, refs = *refs[:3], refs[3:]
    kv_refs, refs = refs[:n_kv], refs[n_kv:]
    w_ref, u_ref, stat_ref, own_ref, refs = *refs[:4], refs[4:]
    send_refs, (keys, values, samples, scores, slopes, parts) = refs[: n_q - 1], refs[n_q - 1 :]
    total = n_q * count
    factor = LOG2E / math.sqrt(width)
    delta, query_samples = lines[0:1, :], lines[1:2, :]
    n_pieces = w_ref.shape[0]
    block = scores.shape[0]
    n_blocks = n_pieces // block

    def load(ref, index):
        keys[index] = ref[:count, :width]
        values[index] = ref[:count, width:]
        samples[index] = jnp.transpose(ref[count:, :].astype(F32))[:count, :8]

    base = 0
    for ref in kv_refs:
        depth = ref.shape[0]
        if depth <= 4:
            for i in range(depth):
                load(ref.at[i], base + i)
        else:

            @pl.loop(0, depth)
            def _(i, ref=ref, base=base):
                load(ref.at[i], base + i)

        base += depth

    def over_blocks(body, state):
        if n_blocks == 1:
            return body(0, state)
        return lax.fori_loop(0, n_blocks, lambda i, s: body(i * block, s), state)

    def fold(part, combine):
        out = part[0:8]
        for start in range(8, count, 8):
            out = combine(out, part[start : start + 8])
        return out

    def product(left, right, first):
        left = left[pl.ds(first, block)].reshape(block * count, width)
        return dot_nt(left, right[...]).reshape(block, count, total)

    def peak_step(first, peak):
        scores[...] = product(keys, queries, first)
        if n_blocks == 1:
            slopes[...] = product(values, grads, first)
        for piece in range(block):
            live = samples[first + piece][:, 3:4] == query_samples
            masked = jnp.where(live, scores[piece], NEG_FILL)
            scores[piece] = masked
            peak = jnp.maximum(peak, fold(masked, jnp.maximum))
        return peak

    turned = jnp.transpose(keys[:block].reshape(block * count, width))

    peak8 = over_blocks(peak_step, jnp.full((8, total), NEG_FILL, F32))
    peak = jnp.max(peak8, axis=0, keepdims=True)

    def grad_step(first, mass):
        if n_blocks > 1:
            peak_step(first, peak8)
            slopes[...] = product(values, grads, first)
        for piece in range(block):
            weight = jnp.exp2((scores[piece] - peak) * factor)
            w_ref[first + piece] = weight.astype(BF16)
            u_ref[first + piece] = (weight * (slopes[piece] - delta)).astype(BF16)
            mass = mass + fold(weight, jnp.add)
            if n_blocks == 1 and (piece + 1) % 4 == 0:
                rows = 4 * count
                first_row = (piece + 1) * count - rows
                known = u_ref[piece + 1 - 4 : piece + 1].reshape(rows, total)
                left = turned[:, first_row : first_row + rows]
                joins.append(jnp.dot(left, known, preferred_element_type=F32))
        return mass

    joins = []
    mass8 = over_blocks(grad_step, jnp.zeros((8, total), F32))
    mass = jnp.sum(mass8, axis=0, keepdims=True)
    level = peak * factor + jnp.log2(mass)
    stat_ref[...] = jnp.zeros_like(stat_ref)
    stat_ref[0:1, :] = peak * factor
    stat_ref[1:2, :] = level

    def join_step(first, joined):
        rows = block * count
        return joined + dot_tn(
            keys[pl.ds(first, block)].reshape(rows, width),
            u_ref[pl.ds(first, block)].reshape(rows, total),
        )

    if n_blocks == 1:
        joined = functools.reduce(jnp.add, joins)
    else:
        joined = over_blocks(join_step, jnp.zeros((width, total), F32))
    parts[...] = jnp.transpose((joined * (1.0 / mass)).astype(BF16))
    own_ref[...] = parts[line_rows(0, count), :]
    tail_rows = send_refs[0].shape[0] - count
    step = tail_rows // 4
    row = lax.broadcasted_iota(jnp.int32, (tail_rows, LANES), 0)
    tail = jnp.zeros((tail_rows, LANES), F32)
    for index, part in enumerate(split_three(level)):
        for chunk in range(total // LANES):
            line = part[:, chunk * LANES : (chunk + 1) * LANES]
            tail = jnp.where(row == index * step + chunk, line, tail)
    for offset, ref in enumerate(send_refs, 1):
        ref[:count, :] = parts[line_rows(offset, count), :]
        ref[count:, :] = tail.astype(BF16)


def products(w_ref, u_ref, first, size, places, queries, grads, key_ref, value_ref, scale):
    _, count, total = w_ref.shape
    many, shape = (size * count, total), (size, count, key_ref.shape[2])
    value_part = jnp.dot(
        w_ref[pl.ds(first, size)].reshape(many), grads[...], preferred_element_type=F32
    ).reshape(shape)
    key_part = jnp.dot(
        u_ref[pl.ds(first, size)].reshape(many), queries[...], preferred_element_type=F32
    ).reshape(shape)
    for step, place in enumerate(places):
        key_ref[place] = (key_part[step] * scale).astype(key_ref.dtype)
        value_ref[place] = value_part[step].astype(value_ref.dtype)


def away_kernel(count, width, n_q, plane, n_y, *refs):
    w_ref, u_ref, stat_ref, all_queries, all_grads, refs = *refs[:5], refs[5:]
    got_refs, refs = refs[: n_q - 1][::-1], refs[n_q - 1 :]
    other_k_ref, other_v_ref, queries, grads, shares_ref, table = refs
    chunks = n_q * count // LANES
    scale = 1.0 / math.sqrt(width)
    levels = [stat_ref[1:2, :]]
    for ref in got_refs:
        tail = ref[count:, :].astype(F32)
        step = tail.shape[0] // 4
        summed = tail[:step] + tail[step : 2 * step] + tail[2 * step : 3 * step]
        levels.append(jnp.concatenate([summed[c : c + 1] for c in range(chunks)], axis=1))
    top = functools.reduce(jnp.maximum, levels)
    shares = [jnp.exp2(one - top) for one in levels]
    inverse = 1.0 / functools.reduce(jnp.add, shares)
    table[...] = jnp.zeros_like(table)
    table[0:1, :] = jnp.exp2(stat_ref[0:1, :] - top) * inverse
    for index, share in enumerate(shares, 1):
        table[index : index + 1, :] = share * inverse * scale
    columns = jnp.transpose(table[...])
    shares_ref[...] = columns
    queries[...] = (all_queries[...].astype(F32) * columns[:, 0:1]).astype(BF16)
    grads[...] = (all_grads[...].astype(F32) * columns[:, 0:1]).astype(BF16)
    half = w_ref.shape[0] // 2
    places = plane_places(plane, n_y)
    if half <= 4:
        products(
            w_ref, u_ref, half, half, places, queries, grads, other_k_ref, other_v_ref, scale
        )
    else:
        for i, place in enumerate(places):
            products(
                w_ref, u_ref, half + i, 1, [place], queries, grads, other_k_ref, other_v_ref, scale
            )


def query_kernel(own_ref, shares_ref, *refs):
    *got_refs, low_ref, high_ref = refs
    count, _ = own_ref.shape
    own = shares_ref[line_rows(0, count), :]
    query_grad = own_ref[...].astype(F32) * own[:, 1:2]
    for index, ref in enumerate(got_refs, 2):
        query_grad = query_grad + ref[:count, :].astype(F32) * own[:, index : index + 1]
    cut = low_ref.shape[0]
    low_ref[...] = query_grad[:cut].astype(BF16)
    high_ref[...] = query_grad[cut:].astype(BF16)


def home_kernel(plane, n_y, w_ref, u_ref, queries, grads, key_ref, value_ref):
    half = w_ref.shape[0] // 2
    places = plane_places(plane, n_y)
    scale = 1.0 / math.sqrt(queries.shape[1])
    if half <= 4:
        products(w_ref, u_ref, 0, half, places, queries, grads, key_ref, value_ref, scale)
    else:
        for i, place in enumerate(places):
            products(w_ref, u_ref, i, 1, [place], queries, grads, key_ref, value_ref, scale)


def token_product(plane, n_y, x_refs, g_refs, inputs, grads):
    query_ref, key_ref, value_ref = g_refs
    n_plane = len(plane)
    count, width = key_ref.shape[1:]
    cut = cut_rows(count)
    high, rest = n_plane * cut, count - cut
    core_id = lax.axis_index("core")
    for slot, place in enumerate(plane_places(plane, n_y)):
        rows = slice(slot * count, (slot + 1) * count)
        inputs[rows, :] = x_refs[slot][core_id]
        middle = slot * count + cut
        grads[slot * count : middle, :width] = query_ref[slot * cut : (slot + 1) * cut, :]
        grads[middle : (slot + 1) * count, :width] = query_ref[
            high + slot * rest : high + (slot + 1) * rest, :
        ]
        grads[rows, width : 2 * width] = key_ref[place]
        grads[rows, 2 * width :] = value_ref[place]
    return dot_tn(inputs[...], grads[...])


def near_kernel(plane, n_y, *refs):
    x_refs, g_refs = refs[: len(plane)], refs[len(plane) : len(plane) + 3]
    sum_ref, inputs, grads = refs[len(plane) + 3 :]
    sum_ref[...] = token_product(plane, n_y, x_refs, g_refs, inputs, grads)


def far_kernel(plane, n_y, n_z, near_ref, *refs):
    x_refs, g_refs = refs[: len(plane)], refs[len(plane) : len(plane) + 3]
    refs = refs[len(plane) + 3 :]
    out_refs, (inputs, grads, sums) = refs[:n_z], refs[n_z:]
    total = near_ref[...] + token_product(plane, n_y, x_refs, g_refs, inputs, grads)
    sums[...] = total.reshape(sums.shape)
    z_id = lax.axis_index("z")
    for slot, ref in enumerate(out_refs):
        ref[...] = sums[z_id ^ slot].astype(ref.dtype)


def xor_permute(value, names, offsets):
    sizes = [lax.axis_size(name) for name in names]
    pairs = []
    for source in range(math.prod(sizes)):
        rest, digits = source, []
        for size in reversed(sizes):
            digits.append(rest % size)
            rest //= size
        target = 0
        for digit, size, offset in zip(reversed(digits), sizes, offsets):
            target = target * size + (digit ^ offset)
        pairs.append((source, target))
    return lax.ppermute(value, tuple(names), pairs)


def local(axes, layer_input, queries, keys, values, forward_out, out_grad, token_pos, block_sample):
    sizes = dict(axes)
    n_row, n_z, n_y, n_core = (sizes[name] for name in ("row", "z", "y", "core"))
    count, width = queries.shape
    model_width = layer_input.shape[1]
    total = n_z * count
    plane = [(a, b) for a in range(n_row) for b in range(n_y)]
    n_plane = len(plane)
    n_pieces = n_core * n_plane

    def over_plane(value, where):
        return xor_permute(value, ("row", "y"), where)

    def over_z(values):
        far_first = reversed(list(enumerate(values, 1)))
        return [xor_permute(value, ("z",), (offset,)) for offset, value in far_first][::-1]

    def over_core(value):
        return xor_permute(value, ("core",), (1,))

    packed = jax.ShapeDtypeStruct((count + PAD_ROWS, 2 * width), BF16)
    x_here = layer_input
    qg, kv = pl.pallas_call(
        functools.partial(pack_kernel, axes),
        out_shape=(packed, packed),
        in_specs=[HBM] * 7,
        out_specs=(VMEM, VMEM),
        scratch_shapes=[
            pltpu.VMEM((count, width), BF16),
            pltpu.VMEM((2 * width, width), F32),
            pltpu.VMEM((PAD_ROWS, 2 * width), F32),
            pltpu.VMEM((token_pos.shape[0] // LANES, LANES), jnp.int32),
            pltpu.SMEM(block_sample.shape, jnp.int32),
            pltpu.SemaphoreType.DMA((7,)),
        ],
        compiler_params=params(8 * MIB),
        name="pack",
    )(
        *(
            pltpu.with_memory_space_constraint(value, pltpu.HBM)
            for value in (
                queries,
                keys,
                values,
                forward_out,
                out_grad,
                token_pos.reshape(-1, LANES),
                block_sample,
            )
        )
    )

    blk = model_width // (n_z * n_y * n_core * n_row)
    kv_near = [kv] + [over_plane(kv, where) for where in plane[1:]]
    qg_all = [qg] + over_z([qg] * (n_z - 1))
    x_here, kv_near[1:] = lax.optimization_barrier((x_here, kv_near[1:]))
    x_send = pl.pallas_call(
        functools.partial(deal_kernel, (n_row, n_z, n_y, n_core)),
        out_shape=[jax.ShapeDtypeStruct((n_core, count, n_z * blk), BF16)] * n_plane,
        in_specs=[HBM],
        out_specs=[VMEM] * n_plane,
        scratch_shapes=[
            pltpu.VMEM((n_plane, n_core, count, n_z * blk), BF16),
            pltpu.VMEM(layer_input.shape, BF16),
            pltpu.SemaphoreType.DMA(()),
        ],
        compiler_params=params(16 * MIB),
        name="deal",
    )(pltpu.with_memory_space_constraint(x_here, pltpu.HBM))
    stacked = jnp.stack(kv_near)
    kv_all = [piece[None] for piece in kv_near] if n_pieces <= 8 else [stacked]
    kv_all = kv_all + [over_core(stacked)]

    tail_rows = 4 * -(-total // (8 * LANES)) * 8
    big = jax.ShapeDtypeStruct((n_pieces, count, total), BF16)
    lines = pl.pallas_call(
        functools.partial(lines_kernel, count, width, n_z),
        out_shape=[jax.ShapeDtypeStruct((total, width), BF16)] * 2
        + [jax.ShapeDtypeStruct((8, total), F32)],
        in_specs=[VMEM] * n_z,
        out_specs=[VMEM] * 3,
        compiler_params=params(8 * MIB),
        cost_estimate=pl.CostEstimate(flops=int(5e9), bytes_accessed=0, transcendentals=0),
        name="lines",
    )(*qg_all[::-1])
    w, u, stat, own_part, *send = pl.pallas_call(
        functools.partial(forward_kernel, count, width, n_z, len(kv_all)),
        out_shape=[
            big,
            big,
            jax.ShapeDtypeStruct((8, total), F32),
            jax.ShapeDtypeStruct((count, width), BF16),
        ]
        + [jax.ShapeDtypeStruct((count + tail_rows, width), BF16)] * (n_z - 1),
        in_specs=[VMEM] * (3 + len(kv_all)),
        out_specs=[VMEM] * (4 + n_z - 1),
        scratch_shapes=[
            pltpu.VMEM((n_pieces, count, width), BF16),
            pltpu.VMEM((n_pieces, count, width), BF16),
            pltpu.VMEM((n_pieces, count, 8), F32),
            pltpu.VMEM((math.gcd(n_pieces, 8), count, total), F32),
            pltpu.VMEM((math.gcd(n_pieces, 8), count, total), F32),
            pltpu.VMEM((total, width), BF16),
        ],
        compiler_params=params(24 * MIB if n_pieces <= 8 else 56 * MIB),
        cost_estimate=pl.CostEstimate(flops=int(3e10), bytes_accessed=0, transcendentals=0),
        name="forward",
    )(*lines, *kv_all)
    got = over_z(send)
    x_all = [x_send[0]] + [over_plane(x, where) for x, where in zip(x_send[1:], plane[1:])]
    far = [index for index, (a, b) in enumerate(plane) if a and b]
    near = [index for index, (a, b) in enumerate(plane) if (a or b) and not (a and b)]

    def together(values, indices):
        values, some = lax.optimization_barrier((values, [x_all[index] for index in indices]))
        for index, value in zip(indices, some):
            x_all[index] = value
        return values

    got = together(got, far)

    half = (n_plane, count, width)
    cut = cut_rows(count)
    other_k, other_v, queries_low, grads_low, shares = pl.pallas_call(
        functools.partial(away_kernel, count, width, n_z, plane, n_y),
        out_shape=[jax.ShapeDtypeStruct(half, BF16)] * 2
        + [jax.ShapeDtypeStruct((total, width), BF16)] * 2
        + [jax.ShapeDtypeStruct((total, 8), F32)],
        in_specs=[VMEM] * (5 + n_z - 1),
        out_specs=[VMEM] * 5,
        scratch_shapes=[pltpu.VMEM((8, total), F32)],
        compiler_params=params(16 * MIB if n_pieces <= 8 else 56 * MIB),
        cost_estimate=pl.CostEstimate(flops=int(3e10), bytes_accessed=0, transcendentals=0),
        name="away",
    )(w, u, stat, *lines[:2], *got[::-1])
    query_low, query_high = pl.pallas_call(
        query_kernel,
        out_shape=[
            jax.ShapeDtypeStruct((cut, width), BF16),
            jax.ShapeDtypeStruct((count - cut, width), BF16),
        ],
        in_specs=[VMEM] * (2 + n_z - 1),
        out_specs=[VMEM] * 2,
        compiler_params=params(8 * MIB),
        name="query",
    )(own_part, shares, *got)
    mine_k, mine_v = pl.pallas_call(
        functools.partial(home_kernel, plane, n_y),
        out_shape=[jax.ShapeDtypeStruct(half, F32 if n_pieces <= 8 else BF16)] * 2,
        in_specs=[VMEM] * 4,
        out_specs=[VMEM] * 2,
        compiler_params=params(16 * MIB if n_pieces <= 8 else 56 * MIB),
        name="home",
    )(w, u, queries_low, grads_low)
    mine_k, mine_v = together([mine_k, mine_v], near)
    key_sum = mine_k.astype(F32) + over_core(other_k).astype(F32)
    value_sum = mine_v.astype(F32) + over_core(other_v).astype(F32)
    x_pair = [over_core(x) for x in x_all]
    row_bits = [(1 << bit, 0) for bit in range(n_row.bit_length() - 1)]
    y_bits = [(0, 1 << bit) for bit in range(n_y.bit_length() - 1)]
    lows, highs = {(0, 0): query_low}, {(0, 0): query_high}
    body = n_plane * count

    def payload(sums, pieces):
        return jnp.concatenate([sums.astype(BF16).reshape(body, width), *pieces.values()])

    def take(sums, pieces, got, hop, rows):
        for index, (a, b) in enumerate(list(pieces)):
            first = body + index * rows
            pieces[a ^ hop[0], b ^ hop[1]] = got[first : first + rows]
        return sums + got[:body].reshape(half).astype(F32)

    for key_hop, value_hop in zip(row_bits + y_bits, y_bits + row_bits):
        sent = lax.optimization_barrier((payload(key_sum, lows), payload(value_sum, highs)))
        key_got, value_got = lax.optimization_barrier(
            (over_plane(sent[0], key_hop), over_plane(sent[1], value_hop))
        )
        key_sum = take(key_sum, lows, key_got, key_hop, cut)
        value_sum = take(value_sum, highs, value_got, value_hop, count - cut)
    place = plane_places(plane, n_y)[0]
    key_low, value_low = key_sum.astype(BF16), value_sum.astype(BF16)
    key_grad = lax.dynamic_index_in_dim(key_low, place, 0, False)
    value_grad = lax.dynamic_index_in_dim(value_low, place, 0, False)
    query_all = [pieces[where] for pieces in (lows, highs) for where in plane]
    g_near = [jnp.concatenate(query_all), key_low, value_low]
    g_far = [over_core(g) for g in g_near]

    tokens = n_plane * count
    operands = [pltpu.VMEM((tokens, n_z * blk), BF16), pltpu.VMEM((tokens, 3 * width), BF16)]
    near_sum = pl.pallas_call(
        functools.partial(near_kernel, plane, n_y),
        out_shape=jax.ShapeDtypeStruct((n_z * blk, 3 * width), F32),
        in_specs=[VMEM] * (n_plane + 3),
        out_specs=VMEM,
        scratch_shapes=operands,
        compiler_params=params(24 * MIB),
        name="near",
    )(*x_all, *g_near)
    mine, *send = pl.pallas_call(
        functools.partial(far_kernel, plane, n_y, n_z),
        out_shape=[jax.ShapeDtypeStruct((blk, 3 * width), F32)]
        + [jax.ShapeDtypeStruct((blk, 3 * width), BF16)] * (n_z - 1),
        in_specs=[VMEM] * (n_plane + 4),
        out_specs=[VMEM] * n_z,
        scratch_shapes=operands + [pltpu.VMEM((n_z, blk, 3 * width), F32)],
        compiler_params=params(24 * MIB),
        name="far",
    )(near_sum, *x_pair, *g_far)
    mine, query_low, query_high = lax.optimization_barrier((mine, query_low, query_high))
    both = [mine] + send
    piece = both[0]
    for part in over_z(both[1:]):
        piece = piece + part.astype(F32)
    low = piece.astype(BF16)
    parts = [piece] + [xor_permute(low, ("row",), (a,)) for a in range(1, n_row)]
    weight_grad = pl.pallas_call(
        assemble_kernel,
        out_shape=jax.ShapeDtypeStruct((n_row, blk, 3 * width), F32),
        in_specs=[VMEM] * n_row,
        out_specs=VMEM,
        compiler_params=params(8 * MIB),
        name="assemble",
    )(*parts).reshape(n_row * blk, 3 * width)
    query_grad = jnp.concatenate([query_low, query_high])
    return query_grad, key_grad, value_grad, weight_grad


def solution(mesh):
    n_row, n_col = mesh.shape["row"], mesh.shape["col"]
    n_core = 2
    n_z = 1 << ((n_col.bit_length() - 1) // 2)
    n_y = n_col // (n_core * n_z)
    axes = (("row", n_row), ("z", n_z), ("y", n_y), ("core", n_core))
    split = Mesh(
        mesh.devices.reshape(tuple(size for _, size in axes)), tuple(name for name, _ in axes)
    )
    tokens = P(("row", "z", "y", "core"), None)
    return jax.shard_map(
        functools.partial(local, axes),
        mesh=split,
        in_specs=(tokens,) * 6 + (P(), P()),
        out_specs=(tokens, tokens, tokens, P(("z", "y", "core"), None)),
        check_vma=False,
    )
```

```python
import functools
import math

import jax
import jax.numpy as jnp
from jax import lax
from jax.experimental import pallas as pl
from jax.experimental.pallas import tpu as pltpu
from jax.sharding import Mesh
from jax.sharding import PartitionSpec as P

BLK = 128
LANES = 128
PAD_ROWS = 16
NEG_FILL = -1e30
LOG2E = math.log2(math.e)
MIB = 1 << 20
F32 = jnp.float32
BF16 = jnp.bfloat16
VMEM = pl.BlockSpec(memory_space=pltpu.VMEM)
HBM = pl.BlockSpec(memory_space=pltpu.HBM)


def cut_rows(count):
    return count * 9 // (10 * PAD_ROWS) * PAD_ROWS


def plane_places(plane, n_y):
    row_id, y_id = lax.axis_index("row"), lax.axis_index("y")
    return [(row_id ^ a) * n_y + (y_id ^ b) for a, b in plane]


def dot_nt(left, right, precision=None):
    return lax.dot_general(
        left, right, (((1,), (1,)), ((), ())), preferred_element_type=F32, precision=precision
    )


def dot_tn(left, right):
    return lax.dot_general(left, right, (((0,), (0,)), ((), ())), preferred_element_type=F32)


def params(nbytes):
    return pltpu.CompilerParams(vmem_limit_bytes=nbytes)


def split_three(values):
    high = values.astype(BF16).astype(F32)
    rest = values - high
    middle = rest.astype(BF16).astype(F32)
    return high, middle, rest - middle


def pack_kernel(
    axes, q_hbm, k_hbm, v_hbm, o_hbm, g_hbm, pos_hbm, ids_hbm, qg_ref, kv_ref, *scratch
):
    outs, prod, extra, pos, ids, sems = scratch
    count, width = outs.shape
    copies = [
        pltpu.make_async_copy(source, target, sems.at[place])
        for place, (source, target) in enumerate(
            (
                (pos_hbm, pos),
                (ids_hbm, ids),
                (g_hbm, qg_ref.at[:count, width:]),
                (o_hbm, outs),
                (q_hbm, qg_ref.at[:count, :width]),
                (k_hbm, kv_ref.at[:count, :width]),
                (v_hbm, kv_ref.at[:count, width:]),
            )
        )
    ]
    for copy in copies:
        copy.start()
    me = jnp.int32(0)
    for name, size in axes:
        me = me * size + lax.axis_index(name)
    prod[...] = jnp.zeros_like(prod)
    copies[0].wait()
    copies[1].wait()
    lines = min(pos.shape[0], (count + LANES - 2) // LANES + 1)
    first = jnp.minimum(me * count // LANES, pos.shape[0] - lines)
    shift = me * count - first * LANES
    block = jnp.concatenate([pos[pl.ds(first + i, 1), :] for i in range(lines)], axis=1) // BLK

    def add_id(index, found):
        return jnp.where(block == index, ids[index], found)

    found = lax.fori_loop(0, ids.shape[0], add_id, jnp.zeros_like(block), unroll=8)
    found = jnp.broadcast_to(found.astype(F32), (8, lines * LANES))
    found = pltpu.roll(found, lines * LANES - shift, 1)
    copies[2].wait()
    copies[3].wait()
    prod[:count, :] = qg_ref[:count, width:].astype(F32) * outs[...].astype(F32)
    delta = dot_nt(
        jnp.ones((PAD_ROWS, width), F32), prod[...], precision=lax.Precision.HIGHEST
    )
    high, middle, low = split_three(delta)
    row = lax.broadcasted_iota(jnp.int32, delta.shape, 0)
    extra[...] = jnp.where(row == 0, high, jnp.where(row == 1, middle, jnp.where(row == 2, low, 0.0)))
    extra[3:4, :count] = found[0:1, :count]
    tail = extra[...].astype(BF16)
    qg_ref[count:, :] = tail
    kv_ref[count:, :] = tail
    for copy in copies[4:]:
        copy.wait()


def deal_kernel(sizes, x_hbm, *refs):
    *out_refs, dealt, x_ref, sem = refs
    copy = pltpu.make_async_copy(x_hbm, x_ref, sem)
    copy.start()
    copy.wait()
    n_row, n_z, n_y, n_core = sizes
    blk = x_ref.shape[1] // (n_row * n_z * n_y * n_core)
    for a in range(n_row):
        for b in range(n_y):
            for core in range(n_core):
                for z in range(n_z):
                    first = (((z * n_y + b) * n_core + core) * n_row + a) * blk
                    dealt[a * n_y + b, core, :, z * blk : (z + 1) * blk] = x_ref[:, first : first + blk]
    me_row, me_y = lax.axis_index("row"), lax.axis_index("y")
    for a in range(n_row):
        for b in range(n_y):
            out_refs[a * n_y + b][...] = dealt[(me_row ^ a) * n_y + (me_y ^ b)]


def assemble_kernel(own_ref, *refs):
    *got_refs, out_ref = refs
    me_row = lax.axis_index("row")
    out_ref[me_row] = own_ref[...]
    for offset, ref in enumerate(got_refs, 1):
        out_ref[me_row ^ offset] = ref[...].astype(F32)


def line_rows(slot, count):
    place = lax.axis_index("z") ^ slot
    return pl.ds(pl.multiple_of(place * count, PAD_ROWS), count)


def lines_kernel(count, width, n_q, *refs):
    qg_refs, (queries, grads, rows) = refs[:n_q][::-1], refs[n_q:]
    z_id = lax.axis_index("z")
    for slot, ref in enumerate(qg_refs):
        queries[line_rows(slot, count), :] = ref[:count, :width]
        grads[line_rows(slot, count), :] = ref[:count, width:]
    tails = [ref[count:, :].astype(F32) for ref in qg_refs]
    deltas = [(tail[0:1] + tail[1:2] + tail[2:3])[:, :count] for tail in tails]
    samples = [tail[3:4, :count] for tail in tails]
    for place in range(n_q):
        where = slice(place * count, (place + 1) * count)
        delta, sample = deltas[0], samples[0]
        for slot in range(1, n_q):
            here = (z_id ^ slot) == place
            delta = jnp.where(here, deltas[slot], delta)
            sample = jnp.where(here, samples[slot], sample)
        rows[0:1, where] = delta
        rows[1:2, where] = sample


def forward_kernel(count, width, n_q, n_kv, *refs):
    queries, grads, lines, refs = *refs[:3], refs[3:]
    kv_refs, refs = refs[:n_kv], refs[n_kv:]
    w_ref, u_ref, stat_ref, own_ref, refs = *refs[:4], refs[4:]
    send_refs, (keys, values, samples, scores, slopes, parts) = refs[: n_q - 1], refs[n_q - 1 :]
    total = n_q * count
    factor = LOG2E / math.sqrt(width)
    delta, query_samples = lines[0:1, :], lines[1:2, :]
    n_pieces = w_ref.shape[0]
    block = scores.shape[0]
    n_blocks = n_pieces // block

    def load(ref, index):
        keys[index] = ref[:count, :width]
        values[index] = ref[:count, width:]
        samples[index] = jnp.transpose(ref[count:, :].astype(F32))[:count, :8]

    base = 0
    for ref in kv_refs:
        depth = ref.shape[0]
        if depth <= 4:
            for i in range(depth):
                load(ref.at[i], base + i)
        else:

            @pl.loop(0, depth)
            def _(i, ref=ref, base=base):
                load(ref.at[i], base + i)

        base += depth

    def over_blocks(body, state):
        if n_blocks == 1:
            return body(0, state)
        return lax.fori_loop(0, n_blocks, lambda i, s: body(i * block, s), state)

    def fold(part, combine):
        out = part[0:8]
        for start in range(8, count, 8):
            out = combine(out, part[start : start + 8])
        return out

    def product(left, right, first):
        left = left[pl.ds(first, block)].reshape(block * count, width)
        return dot_nt(left, right[...]).reshape(block, count, total)

    def peak_step(first, peak):
        scores[...] = product(keys, queries, first)
        if n_blocks == 1:
            slopes[...] = product(values, grads, first)
        for piece in range(block):
            live = samples[first + piece][:, 3:4] == query_samples
            masked = jnp.where(live, scores[piece], NEG_FILL)
            scores[piece] = masked
            peak = jnp.maximum(peak, fold(masked, jnp.maximum))
        return peak

    turned = jnp.transpose(keys[:block].reshape(block * count, width))

    peak8 = over_blocks(peak_step, jnp.full((8, total), NEG_FILL, F32))
    peak = jnp.max(peak8, axis=0, keepdims=True)

    def grad_step(first, mass):
        if n_blocks > 1:
            peak_step(first, peak8)
            slopes[...] = product(values, grads, first)
        for piece in range(block):
            weight = jnp.exp2((scores[piece] - peak) * factor)
            w_ref[first + piece] = weight.astype(BF16)
            u_ref[first + piece] = (weight * (slopes[piece] - delta)).astype(BF16)
            mass = mass + fold(weight, jnp.add)
            if n_blocks == 1 and (piece + 1) % 4 == 0:
                rows = 4 * count
                first_row = (piece + 1) * count - rows
                known = u_ref[piece + 1 - 4 : piece + 1].reshape(rows, total)
                left = turned[:, first_row : first_row + rows]
                joins.append(jnp.dot(left, known, preferred_element_type=F32))
        return mass

    joins = []
    mass8 = over_blocks(grad_step, jnp.zeros((8, total), F32))
    mass = jnp.sum(mass8, axis=0, keepdims=True)
    level = peak * factor + jnp.log2(mass)
    stat_ref[...] = jnp.zeros_like(stat_ref)
    stat_ref[0:1, :] = peak * factor
    stat_ref[1:2, :] = level

    def join_step(first, joined):
        rows = block * count
        return joined + dot_tn(
            keys[pl.ds(first, block)].reshape(rows, width),
            u_ref[pl.ds(first, block)].reshape(rows, total),
        )

    if n_blocks == 1:
        joined = functools.reduce(jnp.add, joins)
    else:
        joined = over_blocks(join_step, jnp.zeros((width, total), F32))
    parts[...] = jnp.transpose((joined * (1.0 / mass)).astype(BF16))
    own_ref[...] = parts[line_rows(0, count), :]
    tail_rows = send_refs[0].shape[0] - count
    step = tail_rows // 4
    row = lax.broadcasted_iota(jnp.int32, (tail_rows, LANES), 0)
    tail = jnp.zeros((tail_rows, LANES), F32)
    for index, part in enumerate(split_three(level)):
        for chunk in range(total // LANES):
            line = part[:, chunk * LANES : (chunk + 1) * LANES]
            tail = jnp.where(row == index * step + chunk, line, tail)
    for offset, ref in enumerate(send_refs, 1):
        ref[:count, :] = parts[line_rows(offset, count), :]
        ref[count:, :] = tail.astype(BF16)


def products(w_ref, u_ref, first, size, places, queries, grads, key_ref, value_ref, scale):
    _, count, total = w_ref.shape
    many, shape = (size * count, total), (size, count, key_ref.shape[2])
    value_part = jnp.dot(
        w_ref[pl.ds(first, size)].reshape(many), grads[...], preferred_element_type=F32
    ).reshape(shape)
    key_part = jnp.dot(
        u_ref[pl.ds(first, size)].reshape(many), queries[...], preferred_element_type=F32
    ).reshape(shape)
    for step, place in enumerate(places):
        key_ref[place] = (key_part[step] * scale).astype(key_ref.dtype)
        value_ref[place] = value_part[step].astype(value_ref.dtype)


def away_kernel(count, width, n_q, plane, n_y, *refs):
    w_ref, u_ref, stat_ref, all_queries, all_grads, refs = *refs[:5], refs[5:]
    got_refs, refs = refs[: n_q - 1][::-1], refs[n_q - 1 :]
    other_k_ref, other_v_ref, queries, grads, shares_ref, table = refs
    chunks = n_q * count // LANES
    scale = 1.0 / math.sqrt(width)
    levels = [stat_ref[1:2, :]]
    for ref in got_refs:
        tail = ref[count:, :].astype(F32)
        step = tail.shape[0] // 4
        summed = tail[:step] + tail[step : 2 * step] + tail[2 * step : 3 * step]
        levels.append(jnp.concatenate([summed[c : c + 1] for c in range(chunks)], axis=1))
    top = functools.reduce(jnp.maximum, levels)
    shares = [jnp.exp2(one - top) for one in levels]
    inverse = 1.0 / functools.reduce(jnp.add, shares)
    table[...] = jnp.zeros_like(table)
    table[0:1, :] = jnp.exp2(stat_ref[0:1, :] - top) * inverse
    for index, share in enumerate(shares, 1):
        table[index : index + 1, :] = share * inverse * scale
    columns = jnp.transpose(table[...])
    shares_ref[...] = columns
    queries[...] = (all_queries[...].astype(F32) * columns[:, 0:1]).astype(BF16)
    grads[...] = (all_grads[...].astype(F32) * columns[:, 0:1]).astype(BF16)
    half = w_ref.shape[0] // 2
    places = plane_places(plane, n_y)
    if half <= 4:
        products(
            w_ref, u_ref, half, half, places, queries, grads, other_k_ref, other_v_ref, scale
        )
    else:
        for i, place in enumerate(places):
            products(
                w_ref, u_ref, half + i, 1, [place], queries, grads, other_k_ref, other_v_ref, scale
            )


def query_kernel(own_ref, shares_ref, *refs):
    *got_refs, low_ref, high_ref = refs
    count, _ = own_ref.shape
    own = shares_ref[line_rows(0, count), :]
    query_grad = own_ref[...].astype(F32) * own[:, 1:2]
    for index, ref in enumerate(got_refs, 2):
        query_grad = query_grad + ref[:count, :].astype(F32) * own[:, index : index + 1]
    cut = low_ref.shape[0]
    low_ref[...] = query_grad[:cut].astype(BF16)
    high_ref[...] = query_grad[cut:].astype(BF16)


def home_kernel(plane, n_y, w_ref, u_ref, queries, grads, key_ref, value_ref):
    half = w_ref.shape[0] // 2
    places = plane_places(plane, n_y)
    scale = 1.0 / math.sqrt(queries.shape[1])
    if half <= 4:
        products(w_ref, u_ref, 0, half, places, queries, grads, key_ref, value_ref, scale)
    else:
        for i, place in enumerate(places):
            products(w_ref, u_ref, i, 1, [place], queries, grads, key_ref, value_ref, scale)


def token_product(plane, n_y, x_refs, g_refs, inputs, grads):
    query_ref, key_ref, value_ref = g_refs
    n_plane = len(plane)
    count, width = key_ref.shape[1:]
    cut = cut_rows(count)
    high, rest = n_plane * cut, count - cut
    core_id = lax.axis_index("core")
    for slot, place in enumerate(plane_places(plane, n_y)):
        rows = slice(slot * count, (slot + 1) * count)
        inputs[rows, :] = x_refs[slot][core_id]
        middle = slot * count + cut
        grads[slot * count : middle, :width] = query_ref[slot * cut : (slot + 1) * cut, :]
        grads[middle : (slot + 1) * count, :width] = query_ref[
            high + slot * rest : high + (slot + 1) * rest, :
        ]
        grads[rows, width : 2 * width] = key_ref[place]
        grads[rows, 2 * width :] = value_ref[place]
    return dot_tn(inputs[...], grads[...])


def near_kernel(plane, n_y, *refs):
    x_refs, g_refs = refs[: len(plane)], refs[len(plane) : len(plane) + 3]
    sum_ref, inputs, grads = refs[len(plane) + 3 :]
    sum_ref[...] = token_product(plane, n_y, x_refs, g_refs, inputs, grads)


def far_kernel(plane, n_y, n_z, near_ref, *refs):
    x_refs, g_refs = refs[: len(plane)], refs[len(plane) : len(plane) + 3]
    refs = refs[len(plane) + 3 :]
    out_refs, (inputs, grads, sums) = refs[:n_z], refs[n_z:]
    total = near_ref[...] + token_product(plane, n_y, x_refs, g_refs, inputs, grads)
    sums[...] = total.reshape(sums.shape)
    z_id = lax.axis_index("z")
    for slot, ref in enumerate(out_refs):
        ref[...] = sums[z_id ^ slot].astype(ref.dtype)


def xor_permute(value, names, offsets):
    sizes = [lax.axis_size(name) for name in names]
    pairs = []
    for source in range(math.prod(sizes)):
        rest, digits = source, []
        for size in reversed(sizes):
            digits.append(rest % size)
            rest //= size
        target = 0
        for digit, size, offset in zip(reversed(digits), sizes, offsets):
            target = target * size + (digit ^ offset)
        pairs.append((source, target))
    return lax.ppermute(value, tuple(names), pairs)


def local(axes, layer_input, queries, keys, values, forward_out, out_grad, token_pos, block_sample):
    sizes = dict(axes)
    n_row, n_z, n_y, n_core = (sizes[name] for name in ("row", "z", "y", "core"))
    count, width = queries.shape
    model_width = layer_input.shape[1]
    total = n_z * count
    plane = [(a, b) for a in range(n_row) for b in range(n_y)]
    n_plane = len(plane)
    n_pieces = n_core * n_plane

    def over_plane(value, where):
        return xor_permute(value, ("row", "y"), where)

    def over_z(values):
        far_first = reversed(list(enumerate(values, 1)))
        return [xor_permute(value, ("z",), (offset,)) for offset, value in far_first][::-1]

    def over_core(value):
        return xor_permute(value, ("core",), (1,))

    packed = jax.ShapeDtypeStruct((count + PAD_ROWS, 2 * width), BF16)
    x_here = layer_input
    qg, kv = pl.pallas_call(
        functools.partial(pack_kernel, axes),
        out_shape=(packed, packed),
        in_specs=[HBM] * 7,
        out_specs=(VMEM, VMEM),
        scratch_shapes=[
            pltpu.VMEM((count, width), BF16),
            pltpu.VMEM((2 * width, width), F32),
            pltpu.VMEM((PAD_ROWS, 2 * width), F32),
            pltpu.VMEM((token_pos.shape[0] // LANES, LANES), jnp.int32),
            pltpu.SMEM(block_sample.shape, jnp.int32),
            pltpu.SemaphoreType.DMA((7,)),
        ],
        compiler_params=params(8 * MIB),
        name="pack",
    )(
        *(
            pltpu.with_memory_space_constraint(value, pltpu.HBM)
            for value in (
                queries,
                keys,
                values,
                forward_out,
                out_grad,
                token_pos.reshape(-1, LANES),
                block_sample,
            )
        )
    )

    blk = model_width // (n_z * n_y * n_core * n_row)
    kv_near = [kv] + [over_plane(kv, where) for where in plane[1:]]
    qg_all = [qg] + over_z([qg] * (n_z - 1))
    x_here, kv_near[1:] = lax.optimization_barrier((x_here, kv_near[1:]))
    x_send = pl.pallas_call(
        functools.partial(deal_kernel, (n_row, n_z, n_y, n_core)),
        out_shape=[jax.ShapeDtypeStruct((n_core, count, n_z * blk), BF16)] * n_plane,
        in_specs=[HBM],
        out_specs=[VMEM] * n_plane,
        scratch_shapes=[
            pltpu.VMEM((n_plane, n_core, count, n_z * blk), BF16),
            pltpu.VMEM(layer_input.shape, BF16),
            pltpu.SemaphoreType.DMA(()),
        ],
        compiler_params=params(16 * MIB),
        name="deal",
    )(pltpu.with_memory_space_constraint(x_here, pltpu.HBM))
    stacked = jnp.stack(kv_near)
    kv_all = [piece[None] for piece in kv_near] if n_pieces <= 8 else [stacked]
    kv_all = kv_all + [over_core(stacked)]

    tail_rows = 4 * -(-total // (8 * LANES)) * 8
    big = jax.ShapeDtypeStruct((n_pieces, count, total), BF16)
    lines = pl.pallas_call(
        functools.partial(lines_kernel, count, width, n_z),
        out_shape=[jax.ShapeDtypeStruct((total, width), BF16)] * 2
        + [jax.ShapeDtypeStruct((8, total), F32)],
        in_specs=[VMEM] * n_z,
        out_specs=[VMEM] * 3,
        compiler_params=params(8 * MIB),
        cost_estimate=pl.CostEstimate(flops=int(3e10), bytes_accessed=0, transcendentals=0),
        name="lines",
    )(*qg_all[::-1])
    w, u, stat, own_part, *send = pl.pallas_call(
        functools.partial(forward_kernel, count, width, n_z, len(kv_all)),
        out_shape=[
            big,
            big,
            jax.ShapeDtypeStruct((8, total), F32),
            jax.ShapeDtypeStruct((count, width), BF16),
        ]
        + [jax.ShapeDtypeStruct((count + tail_rows, width), BF16)] * (n_z - 1),
        in_specs=[VMEM] * (3 + len(kv_all)),
        out_specs=[VMEM] * (4 + n_z - 1),
        scratch_shapes=[
            pltpu.VMEM((n_pieces, count, width), BF16),
            pltpu.VMEM((n_pieces, count, width), BF16),
            pltpu.VMEM((n_pieces, count, 8), F32),
            pltpu.VMEM((math.gcd(n_pieces, 8), count, total), F32),
            pltpu.VMEM((math.gcd(n_pieces, 8), count, total), F32),
            pltpu.VMEM((total, width), BF16),
        ],
        compiler_params=params(24 * MIB if n_pieces <= 8 else 56 * MIB),
        cost_estimate=pl.CostEstimate(flops=int(3e10), bytes_accessed=0, transcendentals=0),
        name="forward",
    )(*lines, *kv_all)
    got = over_z(send)
    x_all = [x_send[0]] + [over_plane(x, where) for x, where in zip(x_send[1:], plane[1:])]
    far = [index for index, (a, b) in enumerate(plane) if a and b]
    near = [index for index, (a, b) in enumerate(plane) if (a or b) and not (a and b)]

    def together(values, indices):
        values, some = lax.optimization_barrier((values, [x_all[index] for index in indices]))
        for index, value in zip(indices, some):
            x_all[index] = value
        return values

    got = together(got, far)

    half = (n_plane, count, width)
    cut = cut_rows(count)
    other_k, other_v, queries_low, grads_low, shares = pl.pallas_call(
        functools.partial(away_kernel, count, width, n_z, plane, n_y),
        out_shape=[jax.ShapeDtypeStruct(half, BF16)] * 2
        + [jax.ShapeDtypeStruct((total, width), BF16)] * 2
        + [jax.ShapeDtypeStruct((total, 8), F32)],
        in_specs=[VMEM] * (5 + n_z - 1),
        out_specs=[VMEM] * 5,
        scratch_shapes=[pltpu.VMEM((8, total), F32)],
        compiler_params=params(16 * MIB if n_pieces <= 8 else 56 * MIB),
        cost_estimate=pl.CostEstimate(flops=int(3e10), bytes_accessed=0, transcendentals=0),
        name="away",
    )(w, u, stat, *lines[:2], *got[::-1])
    query_low, query_high = pl.pallas_call(
        query_kernel,
        out_shape=[
            jax.ShapeDtypeStruct((cut, width), BF16),
            jax.ShapeDtypeStruct((count - cut, width), BF16),
        ],
        in_specs=[VMEM] * (2 + n_z - 1),
        out_specs=[VMEM] * 2,
        compiler_params=params(8 * MIB),
        name="query",
    )(own_part, shares, *got)
    mine_k, mine_v = pl.pallas_call(
        functools.partial(home_kernel, plane, n_y),
        out_shape=[jax.ShapeDtypeStruct(half, F32 if n_pieces <= 8 else BF16)] * 2,
        in_specs=[VMEM] * 4,
        out_specs=[VMEM] * 2,
        compiler_params=params(16 * MIB if n_pieces <= 8 else 56 * MIB),
        name="home",
    )(w, u, queries_low, grads_low)
    mine_k, mine_v = together([mine_k, mine_v], near)
    key_sum = mine_k.astype(F32) + over_core(other_k).astype(F32)
    value_sum = mine_v.astype(F32) + over_core(other_v).astype(F32)
    x_pair = [over_core(x) for x in x_all]
    row_bits = [(1 << bit, 0) for bit in range(n_row.bit_length() - 1)]
    y_bits = [(0, 1 << bit) for bit in range(n_y.bit_length() - 1)]
    lows, highs = {(0, 0): query_low}, {(0, 0): query_high}
    body = n_plane * count

    def payload(sums, pieces):
        return jnp.concatenate([sums.astype(BF16).reshape(body, width), *pieces.values()])

    def take(sums, pieces, got, hop, rows):
        for index, (a, b) in enumerate(list(pieces)):
            first = body + index * rows
            pieces[a ^ hop[0], b ^ hop[1]] = got[first : first + rows]
        return sums + got[:body].reshape(half).astype(F32)

    for key_hop, value_hop in zip(row_bits + y_bits, y_bits + row_bits):
        sent = lax.optimization_barrier((payload(key_sum, lows), payload(value_sum, highs)))
        key_got, value_got = lax.optimization_barrier(
            (over_plane(sent[0], key_hop), over_plane(sent[1], value_hop))
        )
        key_sum = take(key_sum, lows, key_got, key_hop, cut)
        value_sum = take(value_sum, highs, value_got, value_hop, count - cut)
    place = plane_places(plane, n_y)[0]
    key_low, value_low = key_sum.astype(BF16), value_sum.astype(BF16)
    key_grad = lax.dynamic_index_in_dim(key_low, place, 0, False)
    value_grad = lax.dynamic_index_in_dim(value_low, place, 0, False)
    query_all = [pieces[where] for pieces in (lows, highs) for where in plane]
    g_near = [jnp.concatenate(query_all), key_low, value_low]
    g_far = [over_core(g) for g in g_near]

    tokens = n_plane * count
    operands = [pltpu.VMEM((tokens, n_z * blk), BF16), pltpu.VMEM((tokens, 3 * width), BF16)]
    near_sum = pl.pallas_call(
        functools.partial(near_kernel, plane, n_y),
        out_shape=jax.ShapeDtypeStruct((n_z * blk, 3 * width), F32),
        in_specs=[VMEM] * (n_plane + 3),
        out_specs=VMEM,
        scratch_shapes=operands,
        compiler_params=params(24 * MIB),
        name="near",
    )(*x_all, *g_near)
    mine, *send = pl.pallas_call(
        functools.partial(far_kernel, plane, n_y, n_z),
        out_shape=[jax.ShapeDtypeStruct((blk, 3 * width), F32)]
        + [jax.ShapeDtypeStruct((blk, 3 * width), BF16)] * (n_z - 1),
        in_specs=[VMEM] * (n_plane + 4),
        out_specs=[VMEM] * n_z,
        scratch_shapes=operands + [pltpu.VMEM((n_z, blk, 3 * width), F32)],
        compiler_params=params(24 * MIB),
        name="far",
    )(near_sum, *x_pair, *g_far)
    mine, query_low, query_high = lax.optimization_barrier((mine, query_low, query_high))
    both = [mine] + send
    piece = both[0]
    for part in over_z(both[1:]):
        piece = piece + part.astype(F32)
    low = piece.astype(BF16)
    parts = [piece] + [xor_permute(low, ("row",), (a,)) for a in range(1, n_row)]
    weight_grad = pl.pallas_call(
        assemble_kernel,
        out_shape=jax.ShapeDtypeStruct((n_row, blk, 3 * width), F32),
        in_specs=[VMEM] * n_row,
        out_specs=VMEM,
        compiler_params=params(8 * MIB),
        name="assemble",
    )(*parts).reshape(n_row * blk, 3 * width)
    query_grad = jnp.concatenate([query_low, query_high])
    return query_grad, key_grad, value_grad, weight_grad


def solution(mesh):
    n_row, n_col = mesh.shape["row"], mesh.shape["col"]
    n_core = 2
    n_z = 1 << ((n_col.bit_length() - 1) // 2)
    n_y = n_col // (n_core * n_z)
    axes = (("row", n_row), ("z", n_z), ("y", n_y), ("core", n_core))
    split = Mesh(
        mesh.devices.reshape(tuple(size for _, size in axes)), tuple(name for name, _ in axes)
    )
    tokens = P(("row", "z", "y", "core"), None)
    return jax.shard_map(
        functools.partial(local, axes),
        mesh=split,
        in_specs=(tokens,) * 6 + (P(), P()),
        out_specs=(tokens, tokens, tokens, P(("z", "y", "core"), None)),
        check_vma=False,
    )
```
